32 devices in a mesh: node: 2 (over core), slab: 16 (over z, y, x).
Axes of the slice: x: 2, y: 2, z: 4, core: 2. Of those that a mesh axis runs over, the one named last changes fastest.
Arguments:
- adjoint_source: float32 [2, 6, 64, 64, 256], P('node', None, 'slab'), may hold values from -6 to 6
- stencil_coef: float32 [2, 4, 64, 64, 256], P('node', None, 'slab'), may hold values from 0.05 to 0.5
- flux_block: float32 [2, 6, 6], P('node'), may hold values from -1.25 to 1.25
- shape_metric: float32 [2, 6, 64, 64, 256], P('node', None, 'slab'), may hold values from -0.3125 to 0.3125
- wall_force: float32 [2, 64, 256], P('node', 'slab'), may hold values from -8 to 8
Outputs:
- wall_gradient: float32 [64, 256], P('slab', 'node')
The draws below stay inside these ranges and needn't reach their ends.
All inputs are finite; a program needn't handle non-finite values.
Results may differ from the reference program's by a relative error of at most 0.00014.
Values sent between devices are 32-bit elements; how exact they have to be, the bound alone decides.
No kernel may reach another device: no remote copies, remote signals or barrier semaphores. Data moves between devices by JAX's collectives and lax.ppermute only.
A program may use at most 64 MiB of HBM per device.

```python
import math
import jax
import jax.numpy as jnp
from jax import lax

NV = 6
NY = 64
NZ = 256
ITERS = 3
NODES = 2
NX = 64


def draw_wall_force(key, part):
    offset = jax.random.uniform(jax.random.fold_in(key, 11), (NODES, 1, 1), jnp.float32, -2.0, 2.0)
    noise = jnp.clip(jax.random.normal(jax.random.fold_in(key, 12), (NODES, NX, NZ), jnp.float32), -5.0, 5.0)
    return offset + noise


def block_scale(key, shape, shards, low, high):
    gain, own = 1.0, jax.random.fold_in(key, 6)
    for dim, blocks in shards:
        heights = jnp.exp(jax.random.uniform(jax.random.fold_in(own, dim), (blocks,), jnp.float32, low / len(shards), high / len(shards)))
        gain = gain * jnp.repeat(heights, shape[dim] // blocks).reshape([-1 if axis == dim else 1 for axis in range(len(shape))])
    return gain


def bell_draw(key, shape, scale, reach, pieces=(), held_as=jnp.bfloat16):
    factor_of = block_scale(key, shape, pieces, -0.22, 0.18) if pieces else 1.0
    values = jax.random.normal(key, shape, jnp.float32) * scale * factor_of
    return jnp.minimum(jnp.maximum(values, -reach), reach).astype(held_as)


def setup_inputs(seed: int = 0) -> dict:
    key_list = jax.random.split(jax.random.key(seed), 6)
    return {
        "adjoint_source": bell_draw(key_list[0], (NODES, NV, NX, NY, NZ), 1.0, 6.0, ((0, 2), (2, 16)), jnp.float32),
        "stencil_coef": jnp.clip(jnp.exp(math.log(0.5) - 2.3025851 * jax.random.uniform(key_list[1], (NODES, 4, NX, NY, NZ), jnp.float32) ** block_scale(key_list[1], (NODES, 4, NX, NY, NZ), ((0, 2), (2, 16)), -0.2, 0.2)), 0.05, 0.5),
        "flux_block": bell_draw(key_list[2], (NODES, NV, NV), (4 * NV) ** -0.5, 1.25, ((0, 2),), jnp.float32),
        "shape_metric": bell_draw(key_list[3], (NODES, NV, NX, NY, NZ), (NV * NY) ** -0.5, 0.3125, ((0, 2), (2, 16)), jnp.float32),
        "wall_force": draw_wall_force(jax.random.fold_in(key_list[5], 71), 0),
    }


def sweep(psi, source, coef, diag, block):
    padded = jnp.pad(psi, ((0, 0), (1, 1), (1, 1), (1, 1)))
    middle = padded[:, 1:-1, 1:-1, 1:-1]
    coupled = coef[1] * (padded[:, 2:, 1:-1, 1:-1] + padded[:, :-2, 1:-1, 1:-1])
    coupled = coupled + coef[2] * (padded[:, 1:-1, 2:, 1:-1] + padded[:, 1:-1, :-2, 1:-1])
    coupled = coupled + coef[3] * (padded[:, 1:-1, 1:-1, 2:] + padded[:, 1:-1, 1:-1, :-2])
    mixed = jnp.einsum('vw,vxyz->wxyz', block, coupled, precision=lax.Precision.HIGHEST)
    return middle + (source - (diag * middle - mixed)) / diag

def reference(adjoint_source, stencil_coef, flux_block, shape_metric, wall_force):
    sens_list = []
    objective_list = []
    for node_id in range(NODES):
        source = adjoint_source[node_id]
        coef = stencil_coef[node_id]
        diag = 0.5 + coef[0] + 2.4 * (coef[1] + coef[2] + coef[3])
        psi = source / diag
        for step in range(ITERS - 1):
            psi = sweep(psi, source, coef, diag, flux_block[node_id])
        sens_list.append(lax.optimization_barrier(jnp.sum(psi * shape_metric[node_id], axis=(0, 2))))
        objective_list.append(jnp.mean(wall_force[node_id]))
    objective = jnp.stack(objective_list)
    order = jnp.arange(NODES, dtype=jnp.float32)
    weight = jnp.sin(math.pi * (order + 0.5) / NODES)
    weight = weight / jnp.sum(weight)
    mean_value = jnp.sum(weight * objective)
    variance = jnp.sum(weight * (objective - mean_value) ** 2)
    spread = jnp.sqrt(variance + 0.25)
    factor = weight * (1.0 + 2.0 * (objective - mean_value) / spread)
    total = jnp.zeros_like(sens_list[0])
    for node_id in range(NODES):
        total = total + factor[node_id] * sens_list[node_id]
    return total
```

```python
import functools
import math

import jax
import jax.numpy as jnp
from jax import lax
from jax.experimental import pallas as pl
from jax.experimental.pallas import tpu as pltpu
from jax.sharding import PartitionSpec as P

ROWS = 8
COST = {"edge_messages": 4, "halo_terms": 2, "first_sweep": 2, "last_sweep": 1}
LIMIT = {"edge_state": 62}


def call(kernel, name, **kw):
    us, limit = COST.get(name, 0), LIMIT.get(name, 24)
    return pl.pallas_call(
        kernel,
        compiler_params=pltpu.CompilerParams(vmem_limit_bytes=limit * 1024 * 1024),
        cost_estimate=pl.CostEstimate(flops=int(us * 1.1e9), bytes_accessed=0, transcendentals=0),
        name=name,
        **kw,
    )


def f32(*shape):
    return jax.ShapeDtypeStruct(shape, jnp.float32)


VMEM = pl.BlockSpec(memory_space=pltpu.VMEM)
SMEM = pl.BlockSpec(memory_space=pltpu.SMEM)
ANY = pl.BlockSpec(memory_space=pl.ANY)


def edge_of(slot, planes):
    up = lax.rem(lax.axis_index("slab") + slot, 2) == 0
    return jnp.where(up, planes - 1, 0)


def inverse_diag(c):
    return 1.0 / (0.5 + c(0) + 2.4 * (c(1) + c(2) + c(3)))


def shift_sum(p, axis):
    size = p.shape[axis]
    place = lax.broadcasted_iota(jnp.int32, p.shape, axis)
    ahead = jnp.where(place < size - 1, pltpu.roll(p, size - 1, axis), 0.0)
    behind = jnp.where(place > 0, pltpu.roll(p, 1, axis), 0.0)
    return ahead + behind


def edge_kernel(
    s_ref, c_ref, wall_ref, u0, u1, wsum_ref, s_buf, c_buf, u_buf, wall_buf, wsum_buf, c_sems, s_sems, u_sems, wall_sems
):
    nv, nx = s_ref.shape[1:3]
    wall_in = pltpu.make_async_copy(wall_ref.at[0], wall_buf, wall_sems.at[0])
    wall_out = pltpu.make_async_copy(wsum_buf, wsum_ref, wall_sems.at[1])
    wall_in.start()
    edges = [edge_of(slot, nx) for slot in (0, 1)]
    c_copies = [pltpu.make_async_copy(c_ref.at[0, :, e], c_buf.at[j], c_sems.at[j]) for j, e in enumerate(edges)]
    s_copies = [
        [pltpu.make_async_copy(s_ref.at[0, v, e], s_buf.at[j, v], s_sems.at[j, v]) for v in range(nv)]
        for j, e in enumerate(edges)
    ]
    u_copies = [
        [pltpu.make_async_copy(u_buf.at[j, v], u.at[v], u_sems.at[j, v]) for v in range(nv)]
        for j, u in enumerate((u0, u1))
    ]
    for j in (0, 1):
        c_copies[j].start()
        for copy in s_copies[j]:
            copy.start()
    wall_in.wait()
    wall = jnp.sum(jnp.sum(wall_buf[...], axis=0, keepdims=True), axis=1, keepdims=True)
    rows = lax.broadcasted_iota(jnp.int32, wsum_buf.shape, 0)
    wsum_buf[...] = jnp.where(rows == lax.axis_index("node"), wall, 0.0)
    wall_out.start()
    for j in (0, 1):
        c_copies[j].wait()
        inv = inverse_diag(lambda k: c_buf[j, k])
        for v in range(nv):
            s_copies[j][v].wait()
            u_buf[j, v] = s_buf[j, v] * inv
            u_copies[j][v].start()
    wall_out.wait()
    for j in (0, 1):
        for copy in u_copies[j]:
            copy.wait()


def edge_state(source, coef, wall):
    nv, ny, nz = source.shape[1], source.shape[3], source.shape[4]
    return call(
        edge_kernel,
        "edge_state",
        out_shape=(f32(nv, ny, nz),) * 2 + (f32(ROWS, 128),),
        in_specs=[ANY] * 3,
        out_specs=(ANY,) * 3,
        scratch_shapes=[
            pltpu.VMEM((2, nv, ny, nz), jnp.float32),
            pltpu.VMEM((2, 4, ny, nz), jnp.float32),
            pltpu.VMEM((2, nv, ny, nz), jnp.float32),
            pltpu.VMEM(wall.shape[1:], jnp.float32),
            pltpu.VMEM((ROWS, 128), jnp.float32),
            pltpu.SemaphoreType.DMA((2,)),
            pltpu.SemaphoreType.DMA((2, nv)),
            pltpu.SemaphoreType.DMA((2, nv)),
            pltpu.SemaphoreType.DMA((2,)),
        ],
    )(source, coef, wall)


def share(buf, parts, rows, part):
    width = buf.shape[1] // parts
    if parts == 1:
        return buf[pl.ds(0, rows), :]
    node = lax.axis_index("node")
    at = pl.multiple_of((node if part == 0 else 1 - node) * width, width)
    return buf[pl.ds(0, rows), pl.ds(at, width)]


def coupled(c_ref, x, below, here, above):
    q = c_ref[0, 1, x] * (below + above)
    q = q + c_ref[0, 2, x] * shift_sum(here, 0)
    return q + c_ref[0, 3, x] * shift_sum(here, 1)


def mixed(f_ref, w, q):
    mix = f_ref[0, 0, w] * q(0)
    for v in range(1, f_ref.shape[1]):
        mix = mix + f_ref[0, v, w] * q(v)
    return mix


def message_kernel(parts, f_ref, s_ref, c_ref, after, *refs):
    del after
    msgs, (q_ref, p_ref, full) = refs[: 2 * parts], refs[2 * parts :]
    nv, nx, ny, nz = s_ref.shape[1:]
    zero = jnp.zeros((ny, nz), jnp.float32)
    for slot in (0, 1):
        edge = edge_of(slot, nx)
        inner = jnp.where(edge == 0, min(1, nx - 1), max(nx - 2, 0))
        inv = inverse_diag(lambda k: c_ref[0, k, edge])
        inv_inner = inverse_diag(lambda k: c_ref[0, k, inner])
        for v in range(nv):
            p_ref[v] = s_ref[0, v, edge] * inv
            beside = s_ref[0, v, inner] * inv_inner
            q_ref[v] = coupled(c_ref, edge, beside, p_ref[v], zero)
        for w in range(nv):
            full[pl.ds(w * ny, ny), :] = p_ref[w] + inv * mixed(f_ref, w, lambda v: q_ref[v])
        full[pl.ds(nv * ny, ny), :] = c_ref[0, 1, edge] * inv
        for part in range(parts):
            msgs[slot * parts + part][...] = share(full, parts, (nv + 1) * ny, part)


def messages(parts, block, source, coef, after):
    nv, nx, ny, nz = source.shape[1:]
    rows = (nv + 1) * ny
    return call(
        functools.partial(message_kernel, parts),
        "edge_messages",
        out_shape=(f32(rows, nz // parts),) * (2 * parts),
        in_specs=[SMEM] + [VMEM] * 2 + [ANY],
        out_specs=(VMEM,) * (2 * parts),
        scratch_shapes=[pltpu.VMEM((nv, ny, nz), jnp.float32)] * 2 + [pltpu.VMEM((rows, nz), jnp.float32)],
    )(block, source, coef, after)


def first_kernel(parts, f_ref, s_ref, c_ref, m_ref, after, p1_ref, b_ref, sens_ref, *refs):
    del after
    weights, (p0, q_ref, inv_ref, full) = refs[:parts], refs[parts:]
    nv, nx, ny, nz = s_ref.shape[1:]
    zero = jnp.zeros((ny, nz), jnp.float32)
    for v in range(nv):
        p0[v, 0] = zero
        p0[v, nx + 1] = zero

    def start(x, _):
        inv = inverse_diag(lambda k: c_ref[0, k, x])
        inv_ref[x] = inv
        own = zero
        for v in range(nv):
            p = s_ref[0, v, x] * inv
            p0[v, x + 1] = p
            own = own + m_ref[0, v, x] * p
            q_ref[v] = m_ref[0, v, x] * inv
        sens_ref[pl.ds(x, 1), :] = jnp.sum(own, axis=0, keepdims=True)
        for v in range(nv):
            b = f_ref[0, v, 0] * q_ref[0]
            for w in range(1, nv):
                b = b + f_ref[0, v, w] * q_ref[w]
            b_ref[v, x] = b
        return 0

    lax.fori_loop(0, nx, start, 0)

    def first(x, _):
        for v in range(nv):
            q_ref[v] = coupled(c_ref, x, p0[v, x], p0[v, x + 1], p0[v, x + 2])
        for w in range(nv):
            p1_ref[w, x] = p0[w, x + 1] + inv_ref[x] * mixed(f_ref, w, lambda v: q_ref[v])
        return 0

    lax.fori_loop(0, nx, first, 0)

    rows = (nv + 1) * ny
    for slot in (0, 1):
        edge = edge_of(slot, nx)
        total = zero
        for w in range(nv):
            weight = c_ref[0, 1, edge] * b_ref[w, edge]
            full[pl.ds(slot * rows + w * ny, ny), :] = weight
            total = total + weight * mixed(f_ref, w, lambda v: p0[v, edge + 1])
        full[pl.ds(slot * rows + nv * ny, ny), :] = total
    for part, weight in enumerate(weights):
        weight[...] = share(full, parts, full.shape[0], part)


def first_sweep(parts, block, source, coef, metric, after):
    nv, nx, ny, nz = source.shape[1:]
    rows = 2 * (nv + 1) * ny
    return call(
        functools.partial(first_kernel, parts),
        "first_sweep",
        out_shape=(f32(nv, nx, ny, nz), f32(nv, nx, ny, nz), f32(nx, nz)) + (f32(rows, nz // parts),) * parts,
        in_specs=[SMEM] + [VMEM] * 3 + [ANY],
        out_specs=(VMEM,) * (3 + parts),
        scratch_shapes=[
            pltpu.VMEM((nv, nx + 2, ny, nz), jnp.float32),
            pltpu.VMEM((nv, ny, nz), jnp.float32),
            pltpu.VMEM((nx, ny, nz), jnp.float32),
            pltpu.VMEM((rows, nz), jnp.float32),
        ],
    )(block, source, coef, metric, after)


def last_kernel(c_ref, p1_ref, b_ref, base_ref, out_ref):
    nv, nx, ny, nz = b_ref.shape
    zero = jnp.zeros((ny, nz), jnp.float32)
    for x in range(nx):
        along = [zero, zero, zero]
        for v in range(nv):
            b = b_ref[v, x]
            p = p1_ref[v, x]
            beside = [p1_ref[v, at] for at in (x - 1, x + 1) if 0 <= at < nx]
            along[0] = along[0] + b * sum(beside[1:], beside[0])
            along[1] = along[1] + b * shift_sum(p, 0)
            along[2] = along[2] + b * shift_sum(p, 1)
        own = c_ref[0, 1, x] * along[0] + c_ref[0, 2, x] * along[1] + c_ref[0, 3, x] * along[2]
        out_ref[x : x + 1, :] = base_ref[x : x + 1, :] + jnp.sum(own, axis=0, keepdims=True)


def last_sweep(coef, p1, b, base):
    return call(
        last_kernel,
        "last_sweep",
        out_shape=f32(*base.shape),
        in_specs=[VMEM] * 4,
        out_specs=VMEM,
    )(coef, p1, b, base)


def halo_kernel(nodes, f_ref, c_ref, b_ref, sens_in, sums_ref, u0, u1, out_ref, g_ref, acc):
    nv, nx, ny, nz = b_ref.shape
    acc[...] = sens_in[...]
    for slot, u in ((0, u0), (1, u1)):
        edge = edge_of(slot, nx)
        inner = jnp.where(edge == 0, 1, nx - 2)
        rho = c_ref[0, 1, edge] * inverse_diag(lambda k: c_ref[0, k, edge])
        here = [jnp.zeros((ny, nz), jnp.float32)] * 3
        for w in range(nv):
            g_ref[w] = rho * mixed(f_ref, w, lambda v: u[v])
        for w in range(nv):
            g = g_ref[w]
            here[0] = here[0] + b_ref[w, inner] * g
            here[1] = here[1] + b_ref[w, edge] * shift_sum(g, 0)
            here[2] = here[2] + b_ref[w, edge] * shift_sum(g, 1)
        there = c_ref[0, 1, inner] * here[0]
        own = c_ref[0, 2, edge] * here[1] + c_ref[0, 3, edge] * here[2]
        acc[pl.ds(inner, 1), :] += jnp.sum(there, axis=0, keepdims=True)
        acc[pl.ds(edge, 1), :] += jnp.sum(own, axis=0, keepdims=True)
    out_ref[...] = jnp.zeros_like(out_ref)
    out_ref[pl.ds(pl.multiple_of(lax.axis_index("node") * ROWS, ROWS), nx), :] = acc[...]
    out_ref[pl.ds(nodes * ROWS, ROWS), pl.ds(0, 128)] = sums_ref[...]


def halo_terms(nodes, block, coef, b, sens, sums, u0, u1):
    nv, nx, ny, nz = b.shape
    assert 1 < nx <= ROWS
    return call(
        functools.partial(halo_kernel, nodes),
        "halo_terms",
        out_shape=f32((nodes + 1) * ROWS, nz),
        in_specs=[SMEM] + [VMEM] * 6,
        out_specs=VMEM,
        scratch_shapes=[pltpu.VMEM((nv, ny, nz), jnp.float32), pltpu.VMEM((nx, nz), jnp.float32)],
    )(block, coef, b, sens, sums, u0, u1)


def factors(nodes, cells, sums):
    raw = [math.sin(math.pi * (n + 0.5) / nodes) for n in range(nodes)]
    weight = [r / sum(raw) for r in raw]
    objective = [sums[n : n + 1, :] * (1.0 / cells) for n in range(nodes)]
    mean = sum(w * o for w, o in zip(weight, objective))
    variance = sum(w * (o - mean) ** 2 for w, o in zip(weight, objective))
    spread = jnp.sqrt(variance + 0.25)
    return [w * (1.0 + 2.0 * (o - mean) / spread) for w, o in zip(weight, objective)]


def final_kernel(parts, nodes, cells, all_ref, *refs):
    weights, msgs = refs[:parts], refs[parts : 3 * parts]
    out_ref, acc = refs[3 * parts :]
    nx, width = out_ref.shape
    rows = msgs[0].shape[0]
    factor = factors(nodes, cells, all_ref[pl.ds(nodes * ROWS, ROWS), pl.ds(0, 128)])
    node = lax.axis_index("node")
    if parts == 1:
        acc[...] = all_ref[pl.ds(pl.multiple_of(node * ROWS, ROWS), ROWS), :]
    else:
        near = share(all_ref, parts, nodes * ROWS, 0)
        acc[...] = sum(factor[n][:, :1] * near[n * ROWS : (n + 1) * ROWS, :] for n in range(nodes))
    for part in range(parts):
        whose = node if part == 0 else 1 - node
        mine = factor[0]
        for n in range(1, nodes):
            mine = jnp.where(whose == n, factor[n], mine)
        for slot in (0, 1):
            total = weights[part][pl.ds(slot * rows, rows), :] * msgs[slot * parts + part][...]
            total = jnp.sum(total, axis=0, keepdims=True)
            acc[pl.ds(edge_of(slot, nx), 1), :] += total * mine[:, :1] if parts > 1 else total
    out_ref[...] = acc[pl.ds(0, nx), :] * (1.0 if parts > 1 else mine[:, :1])


def final_terms(parts, nodes, cells, nx, everything, weights, msgs):
    width = msgs[0].shape[1]
    return call(
        functools.partial(final_kernel, parts, nodes, cells),
        "final_terms",
        out_shape=f32(nx, width),
        in_specs=[VMEM] * (1 + 3 * parts),
        out_specs=VMEM,
        scratch_shapes=[pltpu.VMEM((ROWS, width), jnp.float32)],
    )(everything, *weights, *msgs)


def swap_pairs(value, slot, part=0):
    count, nodes = lax.axis_size("slab"), lax.axis_size("node")
    pairs = []
    for low in range(slot, count - 1, 2):
        pairs += [(low, low + 1), (low + 1, low)]
    if part == 0:
        return lax.ppermute(value, "slab", pairs)
    cross = [(n * count + a, (1 - n) * count + b) for n in range(nodes) for a, b in pairs]
    return lax.ppermute(value, ("node", "slab"), cross)


def from_partner(value, slab, node=0):
    count, nodes = lax.axis_size("slab"), lax.axis_size("node")
    pairs = [(n * count + i, (n ^ node) * count + (i ^ slab)) for n in range(nodes) for i in range(count)]
    return lax.ppermute(value, ("node", "slab"), pairs)


def sum_steps(count):
    assert count & (count - 1) == 0
    steps = [1 << k for k in range(1, count.bit_length() - 1)]
    return steps + [1 ^ (4 if count > 4 else 0)] if count > 1 else []


def per_device(source, coef, block, metric, wall):
    nodes, slabs = lax.axis_size("node"), lax.axis_size("slab")
    nx = source.shape[2]
    cells = wall.shape[1] * slabs * wall.shape[2]
    parts = 1
    own0, own1, wsum = edge_state(source, coef, wall)
    u0, u1 = swap_pairs(own0, 0), swap_pairs(own1, 1)
    own = messages(parts, block, source, coef, wsum)
    msgs = [swap_pairs(m, k // parts, k % parts) for k, m in enumerate(own)]
    sums = wsum
    for slab in sum_steps(slabs):
        sums = sums + from_partner(sums, slab)
    p1, b, sens, *weights = first_sweep(parts, block, source, coef, metric, own[0])
    sens = last_sweep(coef, p1, b, sens)
    everything = lax.psum(halo_terms(nodes, block, coef, b, sens, sums, u0, u1), "node")
    if parts == 2:
        weights[1] = lax.ppermute(weights[1], "node", [(0, 1), (1, 0)])
        return final_terms(parts, nodes, cells, nx, everything, weights, msgs)
    term = final_terms(parts, nodes, cells, nx, everything, weights, msgs)
    total = lax.psum(term, "node")
    width = term.shape[1] // nodes
    return lax.dynamic_slice_in_dim(total, lax.axis_index("node") * width, width, 1)


def solution(mesh):
    return jax.shard_map(
        per_device,
        mesh=mesh,
        in_specs=(
            P("node", None, "slab", None, None),
            P("node", None, "slab", None, None),
            P("node", None, None),
            P("node", None, "slab", None, None),
            P("node", "slab", None),
        ),
        out_specs=P("slab", "node"),
        check_vma=False,
    )
```

```python
import functools
import math

import jax
import jax.numpy as jnp
from jax import lax
from jax.experimental import pallas as pl
from jax.experimental.pallas import tpu as pltpu
from jax.sharding import PartitionSpec as P

ROWS = 8
COST = {"last_sweep": 1}
LIMIT = {"edge_state": 62}


def call(kernel, name, **kw):
    us, limit = COST.get(name, 0), LIMIT.get(name, 24)
    return pl.pallas_call(
        kernel,
        compiler_params=pltpu.CompilerParams(vmem_limit_bytes=limit * 1024 * 1024),
        cost_estimate=pl.CostEstimate(flops=int(us * 1.1e9), bytes_accessed=0, transcendentals=0),
        name=name,
        **kw,
    )


def f32(*shape):
    return jax.ShapeDtypeStruct(shape, jnp.float32)


VMEM = pl.BlockSpec(memory_space=pltpu.VMEM)
SMEM = pl.BlockSpec(memory_space=pltpu.SMEM)
ANY = pl.BlockSpec(memory_space=pl.ANY)


def edge_of(slot, planes):
    up = lax.rem(lax.axis_index("slab") + slot, 2) == 0
    return jnp.where(up, planes - 1, 0)


def inverse_diag(c):
    return 1.0 / (0.5 + c(0) + 2.4 * (c(1) + c(2) + c(3)))


def shift_sum(p, axis):
    size = p.shape[axis]
    place = lax.broadcasted_iota(jnp.int32, p.shape, axis)
    ahead = jnp.where(place < size - 1, pltpu.roll(p, size - 1, axis), 0.0)
    behind = jnp.where(place > 0, pltpu.roll(p, 1, axis), 0.0)
    return ahead + behind


def edge_kernel(
    s_ref, c_ref, wall_ref, u0, u1, wsum_ref, s_buf, c_buf, wall_buf, c_sems, s_sems, wall_sem
):
    nv, nx = s_ref.shape[1:3]
    edges = [edge_of(slot, nx) for slot in (0, 1)]
    c_copies = [pltpu.make_async_copy(c_ref.at[0, :, e], c_buf.at[j], c_sems.at[j]) for j, e in enumerate(edges)]
    s_copies = [pltpu.make_async_copy(s_ref.at[0, :, e], s_buf.at[j], s_sems.at[j]) for j, e in enumerate(edges)]
    wall_copy = pltpu.make_async_copy(wall_ref.at[0], wall_buf, wall_sem)
    for j in (0, 1):
        c_copies[j].start()
        s_copies[j].start()
    wall_copy.start()
    for j, u in enumerate((u0, u1)):
        c_copies[j].wait()
        inv = inverse_diag(lambda k: c_buf[j, k])
        s_copies[j].wait()
        for v in range(nv):
            u[v] = s_buf[j, v] * inv
    wall_copy.wait()
    wall = jnp.sum(jnp.sum(wall_buf[...], axis=0, keepdims=True), axis=1, keepdims=True)
    rows = lax.broadcasted_iota(jnp.int32, wsum_ref.shape, 0)
    wsum_ref[...] = jnp.where(rows == lax.axis_index("node"), wall, 0.0)


def edge_state(source, coef, wall):
    nv, ny, nz = source.shape[1], source.shape[3], source.shape[4]
    return call(
        edge_kernel,
        "edge_state",
        out_shape=(f32(nv, ny, nz),) * 2 + (f32(ROWS, 128),),
        in_specs=[ANY] * 3,
        out_specs=(VMEM,) * 3,
        scratch_shapes=[
            pltpu.VMEM((2, nv, ny, nz), jnp.float32),
            pltpu.VMEM((2, 4, ny, nz), jnp.float32),
            pltpu.VMEM(wall.shape[1:], jnp.float32),
            pltpu.SemaphoreType.DMA((2,)),
            pltpu.SemaphoreType.DMA((2,)),
            pltpu.SemaphoreType.DMA,
        ],
    )(source, coef, wall)


def share(buf, parts, first, rows, part):
    width = buf.shape[1] // parts
    if parts == 1:
        return buf[pl.ds(first, rows), :]
    node = lax.axis_index("node")
    at = pl.multiple_of((node if part == 0 else 1 - node) * width, width)
    return buf[pl.ds(first, rows), pl.ds(at, width)]


def coupled(c_ref, x, below, here, above):
    q = c_ref[0, 1, x] * (below + above)
    q = q + c_ref[0, 2, x] * shift_sum(here, 0)
    return q + c_ref[0, 3, x] * shift_sum(here, 1)


def mixed(f_ref, w, q):
    mix = f_ref[0, 0, w] * q(0)
    for v in range(1, f_ref.shape[1]):
        mix = mix + f_ref[0, v, w] * q(v)
    return mix


def states_kernel(f_ref, s_ref, c_ref, after, even_ref, odd_ref, q_ref, p_ref):
    del after
    nv, nx, ny, nz = s_ref.shape[1:]
    zero = jnp.zeros((ny, nz), jnp.float32)
    for slot, out in ((0, even_ref), (1, odd_ref)):
        edge = edge_of(slot, nx)
        inner = jnp.where(edge == 0, 1, nx - 2)
        inv = inverse_diag(lambda k: c_ref[0, k, edge])
        inv_inner = inverse_diag(lambda k: c_ref[0, k, inner])
        for v in range(nv):
            p_ref[v] = s_ref[0, v, edge] * inv
            beside = s_ref[0, v, inner] * inv_inner
            q_ref[v] = coupled(c_ref, edge, beside, p_ref[v], zero)
        for w in range(nv):
            out[pl.ds(w * ny, ny), :] = p_ref[w] + inv * mixed(f_ref, w, lambda v: q_ref[v])
        out[pl.ds(nv * ny, ny), :] = c_ref[0, 1, edge] * inv


def edge_states(block, source, coef, after):
    nv, nx, ny, nz = source.shape[1:]
    rows = (nv + 1) * ny
    return call(
        states_kernel,
        "edge_states",
        out_shape=(f32(rows, nz),) * 2,
        in_specs=[SMEM] + [VMEM] * 2 + [ANY],
        out_specs=(VMEM,) * 2,
        scratch_shapes=[pltpu.VMEM((nv, ny, nz), jnp.float32)] * 2,
    )(block, source, coef, after)


def first_kernel(f_ref, s_ref, c_ref, m_ref, after, p1_ref, b_ref, sens_ref, weight_ref, p0, q_ref, inv_ref):
    del after
    nv, nx, ny, nz = s_ref.shape[1:]

    def start(x, _):
        inv = inverse_diag(lambda k: c_ref[0, k, x])
        inv_ref[x] = inv
        own = jnp.zeros((ny, nz), jnp.float32)
        for v in range(nv):
            p = s_ref[0, v, x] * inv
            p0[v, x] = p
            own = own + m_ref[0, v, x] * p
            q_ref[v] = m_ref[0, v, x] * inv
        sens_ref[pl.ds(x, 1), :] = jnp.sum(own, axis=0, keepdims=True)
        for v in range(nv):
            b = f_ref[0, v, 0] * q_ref[0]
            for w in range(1, nv):
                b = b + f_ref[0, v, w] * q_ref[w]
            b_ref[v, x] = b
        return 0

    lax.fori_loop(0, nx, start, 0)

    def first(x, _):
        for v in range(nv):
            q_ref[v] = coupled(c_ref, x, p0[v, x - 1], p0[v, x], p0[v, x + 1])
        for w in range(nv):
            p1_ref[w, x - 1] = p0[w, x] + inv_ref[x] * mixed(f_ref, w, lambda v: q_ref[v])
        return 0

    lax.fori_loop(1, nx - 1, first, 0)

    for slot in (0, 1):
        edge = edge_of(slot, nx)
        total = jnp.zeros((ny, nz), jnp.float32)
        for w in range(nv):
            weight = c_ref[0, 1, edge] * b_ref[w, edge]
            weight_ref[pl.ds((slot * nv + w) * ny, ny), :] = weight
            if slot == 1:
                total = total + weight * mixed(f_ref, w, lambda v: p0[v, edge])
    weight_ref[pl.ds(2 * nv * ny, ny), :] = total


def first_sweep(block, source, coef, metric, after):
    nv, nx, ny, nz = source.shape[1:]
    assert 2 < nx <= ROWS
    rows = (2 * nv + 1) * ny
    return call(
        first_kernel,
        "first_sweep",
        out_shape=(f32(nv, nx - 2, ny, nz), f32(nv, nx, ny, nz), f32(nx, nz), f32(rows, nz)),
        in_specs=[SMEM] + [VMEM] * 3 + [ANY],
        out_specs=(VMEM,) * 4,
        scratch_shapes=[
            pltpu.VMEM((nv, nx, ny, nz), jnp.float32),
            pltpu.VMEM((nv, ny, nz), jnp.float32),
            pltpu.VMEM((nx, ny, nz), jnp.float32),
        ],
    )(block, source, coef, metric, after)


def second_kernel(f_ref, far0, far1, state0, state1, after, whole0, whole1):
    del after
    nv, ny, nz = far0.shape
    for far, state, whole in ((far0, state0, whole0), (far1, state1, whole1)):
        rho = state[pl.ds(nv * ny, ny), :]
        for w in range(nv):
            mix = mixed(f_ref, w, lambda v: far[v])
            whole[pl.ds(w * ny, ny), :] = state[pl.ds(w * ny, ny), :] + rho * mix


def second_states(block, far, states, after):
    nv, ny, nz = far[0].shape
    return call(
        second_kernel,
        "second_states",
        out_shape=(f32(nv * ny, nz),) * 2,
        in_specs=[SMEM] + [VMEM] * 4 + [ANY],
        out_specs=(VMEM,) * 2,
    )(block, *far, *states, after)


def last_kernel(c_ref, inner_ref, whole0, whole1, b_ref, base_ref, out_ref, p1):
    nv, nx, ny, nz = b_ref.shape
    zero = jnp.zeros((ny, nz), jnp.float32)
    for slot, whole in ((0, whole0), (1, whole1)):
        for v in range(nv):
            p1[v, edge_of(slot, nx)] = whole[pl.ds(v * ny, ny), :]

    def state(v, x):
        return inner_ref[v, x - 1] if 0 < x < nx - 1 else p1[v, x]

    for x in range(nx):
        along = [zero, zero, zero]
        for v in range(nv):
            b = b_ref[v, x]
            p = state(v, x)
            beside = [state(v, at) for at in (x - 1, x + 1) if 0 <= at < nx]
            along[0] = along[0] + b * sum(beside[1:], beside[0])
            along[1] = along[1] + b * shift_sum(p, 0)
            along[2] = along[2] + b * shift_sum(p, 1)
        own = c_ref[0, 1, x] * along[0] + c_ref[0, 2, x] * along[1] + c_ref[0, 3, x] * along[2]
        out_ref[x : x + 1, :] = base_ref[x : x + 1, :] + jnp.sum(own, axis=0, keepdims=True)


def last_sweep(coef, inner, edges, b, base):
    return call(
        last_kernel,
        "last_sweep",
        out_shape=f32(*base.shape),
        in_specs=[VMEM] * 6,
        out_specs=VMEM,
        scratch_shapes=[pltpu.VMEM(b.shape, jnp.float32)],
    )(coef, inner, *edges, b, base)


def factors(nodes, cells, sums):
    raw = [math.sin(math.pi * (n + 0.5) / nodes) for n in range(nodes)]
    weight = [r / sum(raw) for r in raw]
    objective = [sums[n : n + 1, :] * (1.0 / cells) for n in range(nodes)]
    mean = sum(w * o for w, o in zip(weight, objective))
    variance = sum(w * (o - mean) ** 2 for w, o in zip(weight, objective))
    spread = jnp.sqrt(variance + 0.25)
    return [w * (1.0 + 2.0 * (o - mean) / spread) for w, o in zip(weight, objective)]


def node_kernel(parts, sens_ref, sums_ref, weight_ref, even_ref, odd_ref, *refs):
    outs, acc = refs[:-1], refs[-1]
    nx, nz = sens_ref.shape
    acc[...] = jnp.zeros_like(acc)
    acc[pl.ds(0, nx), :] = sens_ref[...]
    for k in range(nz // 128):
        acc[pl.ds(ROWS, ROWS), pl.ds(k * 128, 128)] = sums_ref[...]
    first = 0
    for slot, msg in ((0, even_ref), (1, odd_ref)):
        rows = msg.shape[0]
        total = weight_ref[pl.ds(first, rows), :] * msg[...]
        acc[pl.ds(edge_of(slot, nx), 1), :] += jnp.sum(total, axis=0, keepdims=True)
        first += rows
    for part, out in enumerate(outs):
        out[...] = share(acc, parts, 0, 2 * ROWS, part)


def node_terms(parts, sens, sums, weight, even, odd):
    nx, nz = sens.shape
    return call(
        functools.partial(node_kernel, parts),
        "node_terms",
        out_shape=(f32(2 * ROWS, nz // parts),) * parts,
        in_specs=[VMEM] * 5,
        out_specs=(VMEM,) * parts,
        scratch_shapes=[pltpu.VMEM((2 * ROWS, nz), jnp.float32)],
    )(sens, sums, weight, even, odd)


def gradient_kernel(nodes, cells, *refs):
    terms, out_ref = refs[:-1], refs[-1]
    nx = out_ref.shape[0]
    factor = factors(nodes, cells, sum(term[pl.ds(ROWS, ROWS), pl.ds(0, 128)] for term in terms))
    node = lax.axis_index("node")
    total = jnp.zeros(out_ref.shape, jnp.float32)
    for part, term in enumerate(terms):
        whose = node if part == 0 else 1 - node
        scale = factor[0]
        for n in range(1, nodes):
            scale = jnp.where(whose == n, factor[n], scale)
        total = total + term[pl.ds(0, nx), :] * scale[:, :1]
    out_ref[...] = total


def gradient(nodes, cells, nx, terms):
    return call(
        functools.partial(gradient_kernel, nodes, cells),
        "gradient",
        out_shape=f32(nx, terms[0].shape[1]),
        in_specs=[VMEM] * len(terms),
        out_specs=VMEM,
    )(*terms)


def swap_pairs(value, slot, part=0):
    count, nodes = lax.axis_size("slab"), lax.axis_size("node")
    pairs = []
    for low in range(slot, count - 1, 2):
        pairs += [(low, low + 1), (low + 1, low)]
    if part == 0:
        return lax.ppermute(value, "slab", pairs)
    cross = [(n * count + a, (1 - n) * count + b) for n in range(nodes) for a, b in pairs]
    return lax.ppermute(value, ("node", "slab"), cross)


def from_partner(value, slab, node=0):
    count, nodes = lax.axis_size("slab"), lax.axis_size("node")
    pairs = [(n * count + i, (n ^ node) * count + (i ^ slab)) for n in range(nodes) for i in range(count)]
    return lax.ppermute(value, ("node", "slab"), pairs)


def sum_steps(count):
    assert count & (count - 1) == 0
    steps = [1 << k for k in range(1, count.bit_length() - 1)]
    return steps + [1 ^ (4 if count > 4 else 0)]


def other_core(value):
    return lax.ppermute(value, "node", [(0, 1), (1, 0)])


def after(value, *others):
    return lax.optimization_barrier((value, *others))[0]


def per_device(source, coef, block, metric, wall):
    nodes, slabs = lax.axis_size("node"), lax.axis_size("slab")
    nx = source.shape[2]
    cells = wall.shape[1] * slabs * wall.shape[2]
    parts = 2 if nodes == 2 else 1
    *own, sums = edge_state(source, coef, wall)
    far = [swap_pairs(value, slot) for slot, value in enumerate(own)]
    inner, b, base, weight = first_sweep(block, source, coef, metric, sums)
    first, *steps = sum_steps(slabs)
    sums = after(sums + from_partner(sums, first), base)
    early, late = steps[: len(steps) // 2], steps[len(steps) // 2 :]
    for slab in early:
        sums = sums + from_partner(sums, slab)
    states = edge_states(block, source, coef, sums)
    odd = swap_pairs(states[1], 1)
    edges = second_states(block, far, states, sums)
    even = swap_pairs(edges[0], 0)
    sums = after(sums, edges[0])
    for slab in late:
        sums = sums + from_partner(sums, slab)
    if parts == 1:
        sums = lax.psum(sums, "node")
    sens = last_sweep(coef, inner, edges, b, base)
    terms = list(node_terms(parts, sens, sums, weight, even, odd))
    if parts == 2:
        terms[1] = other_core(terms[1])
        return gradient(nodes, cells, nx, terms)
    total = lax.psum(gradient(nodes, cells, nx, terms), "node")
    width = total.shape[1] // nodes
    return lax.dynamic_slice_in_dim(total, lax.axis_index("node") * width, width, 1)


def solution(mesh):
    return jax.shard_map(
        per_device,
        mesh=mesh,
        in_specs=(
            P("node", None, "slab", None, None),
            P("node", None, "slab", None, None),
            P("node", None, None),
            P("node", None, "slab", None, None),
            P("node", "slab", None),
        ),
        out_specs=P("slab", "node"),
        check_vma=False,
    )
```

```python
import functools
import math

import jax
import jax.numpy as jnp
from jax import lax
from jax.experimental import pallas as pl
from jax.experimental.pallas import tpu as pltpu
from jax.sharding import PartitionSpec as P

ROWS = 8
COST = {"last_sweep": 1}
LIMIT = {"edge_state": 62}


def call(kernel, name, **kw):
    us, limit = COST.get(name, 0), LIMIT.get(name, 24)
    return pl.pallas_call(
        kernel,
        compiler_params=pltpu.CompilerParams(vmem_limit_bytes=limit * 1024 * 1024),
        cost_estimate=pl.CostEstimate(flops=int(us * 1.1e9), bytes_accessed=0, transcendentals=0),
        name=name,
        **kw,
    )


def f32(*shape):
    return jax.ShapeDtypeStruct(shape, jnp.float32)


VMEM = pl.BlockSpec(memory_space=pltpu.VMEM)
SMEM = pl.BlockSpec(memory_space=pltpu.SMEM)
ANY = pl.BlockSpec(memory_space=pl.ANY)


def edge_of(slot, planes):
    up = lax.rem(lax.axis_index("slab") + slot, 2) == 0
    return jnp.where(up, planes - 1, 0)


def inverse_diag(c):
    return 1.0 / (0.5 + c(0) + 2.4 * (c(1) + c(2) + c(3)))


def shift_sum(p, axis):
    size = p.shape[axis]
    place = lax.broadcasted_iota(jnp.int32, p.shape, axis)
    ahead = jnp.where(place < size - 1, pltpu.roll(p, size - 1, axis), 0.0)
    behind = jnp.where(place > 0, pltpu.roll(p, 1, axis), 0.0)
    return ahead + behind


def edge_kernel(
    s_ref, c_ref, wall_ref, u0, u1, wsum_ref, s_buf, c_buf, wall_buf, c_sems, s_sems, wall_sem
):
    nv, nx = s_ref.shape[1:3]
    edges = [edge_of(slot, nx) for slot in (0, 1)]
    c_copies = [pltpu.make_async_copy(c_ref.at[0, :, e], c_buf.at[j], c_sems.at[j]) for j, e in enumerate(edges)]
    s_copies = [pltpu.make_async_copy(s_ref.at[0, :, e], s_buf.at[j], s_sems.at[j]) for j, e in enumerate(edges)]
    wall_copy = pltpu.make_async_copy(wall_ref.at[0], wall_buf, wall_sem)
    for j in (0, 1):
        c_copies[j].start()
        s_copies[j].start()
    wall_copy.start()
    for j, u in enumerate((u0, u1)):
        c_copies[j].wait()
        inv = inverse_diag(lambda k: c_buf[j, k])
        s_copies[j].wait()
        for v in range(nv):
            u[v] = s_buf[j, v] * inv
    wall_copy.wait()
    wall = jnp.sum(jnp.sum(wall_buf[...], axis=0, keepdims=True), axis=1, keepdims=True)
    rows = lax.broadcasted_iota(jnp.int32, wsum_ref.shape, 0)
    wsum_ref[...] = jnp.where(rows == lax.axis_index("node"), wall, 0.0)


def edge_state(source, coef, wall):
    nv, ny, nz = source.shape[1], source.shape[3], source.shape[4]
    return call(
        edge_kernel,
        "edge_state",
        out_shape=(f32(nv, ny, nz),) * 2 + (f32(ROWS, 128),),
        in_specs=[ANY] * 3,
        out_specs=(VMEM,) * 3,
        scratch_shapes=[
            pltpu.VMEM((2, nv, ny, nz), jnp.float32),
            pltpu.VMEM((2, 4, ny, nz), jnp.float32),
            pltpu.VMEM(wall.shape[1:], jnp.float32),
            pltpu.SemaphoreType.DMA((2,)),
            pltpu.SemaphoreType.DMA((2,)),
            pltpu.SemaphoreType.DMA,
        ],
    )(source, coef, wall)


def share(buf, parts, first, rows, part):
    width = buf.shape[1] // parts
    if parts == 1:
        return buf[pl.ds(first, rows), :]
    node = lax.axis_index("node")
    at = pl.multiple_of((node if part == 0 else 1 - node) * width, width)
    return buf[pl.ds(first, rows), pl.ds(at, width)]


def coupled(c_ref, x, below, here, above):
    q = c_ref[0, 1, x] * (below + above)
    q = q + c_ref[0, 2, x] * shift_sum(here, 0)
    return q + c_ref[0, 3, x] * shift_sum(here, 1)


def mixed(f_ref, w, q):
    mix = f_ref[0, 0, w] * q(0)
    for v in range(1, f_ref.shape[1]):
        mix = mix + f_ref[0, v, w] * q(v)
    return mix


def states_kernel(f_ref, s_ref, c_ref, after, even_ref, odd_ref, q_ref, p_ref):
    del after
    nv, nx, ny, nz = s_ref.shape[1:]
    zero = jnp.zeros((ny, nz), jnp.float32)
    for slot, out in ((0, even_ref), (1, odd_ref)):
        edge = edge_of(slot, nx)
        inner = jnp.where(edge == 0, 1, nx - 2)
        inv = inverse_diag(lambda k: c_ref[0, k, edge])
        inv_inner = inverse_diag(lambda k: c_ref[0, k, inner])
        for v in range(nv):
            p_ref[v] = s_ref[0, v, edge] * inv
            beside = s_ref[0, v, inner] * inv_inner
            q_ref[v] = coupled(c_ref, edge, beside, p_ref[v], zero)
        for w in range(nv):
            out[pl.ds(w * ny, ny), :] = p_ref[w] + inv * mixed(f_ref, w, lambda v: q_ref[v])
        out[pl.ds(nv * ny, ny), :] = c_ref[0, 1, edge] * inv

def edge_states(block, source, coef, after):
    nv, nx, ny, nz = source.shape[1:]
    rows = (nv + 1) * ny
    return call(
        states_kernel,
        "edge_states",
        out_shape=(f32(rows, nz),) * 2,
        in_specs=[SMEM] + [VMEM] * 2 + [ANY],
        out_specs=(VMEM,) * 2,
        scratch_shapes=[pltpu.VMEM((nv, ny, nz), jnp.float32)] * 2,
    )(block, source, coef, after)


def first_kernel(f_ref, s_ref, c_ref, m_ref, after, p1_ref, b_ref, sens_ref, weight_ref, p0, q_ref, inv_ref):
    del after
    nv, nx, ny, nz = s_ref.shape[1:]

    def start(x, _):
        inv = inverse_diag(lambda k: c_ref[0, k, x])
        inv_ref[x] = inv
        own = jnp.zeros((ny, nz), jnp.float32)
        for v in range(nv):
            p = s_ref[0, v, x] * inv
            p0[v, x] = p
            own = own + m_ref[0, v, x] * p
            q_ref[v] = m_ref[0, v, x] * inv
        sens_ref[pl.ds(x, 1), :] = jnp.sum(own, axis=0, keepdims=True)
        for v in range(nv):
            b = f_ref[0, v, 0] * q_ref[0]
            for w in range(1, nv):
                b = b + f_ref[0, v, w] * q_ref[w]
            b_ref[v, x] = b
        return 0

    lax.fori_loop(0, nx, start, 0)

    def first(x, _):
        for v in range(nv):
            q_ref[v] = coupled(c_ref, x, p0[v, x - 1], p0[v, x], p0[v, x + 1])
        for w in range(nv):
            p1_ref[w, x - 1] = p0[w, x] + inv_ref[x] * mixed(f_ref, w, lambda v: q_ref[v])
        return 0

    lax.fori_loop(1, nx - 1, first, 0)

    for slot in (0, 1):
        edge = edge_of(slot, nx)
        total = jnp.zeros((ny, nz), jnp.float32)
        for w in range(nv):
            weight = c_ref[0, 1, edge] * b_ref[w, edge]
            weight_ref[pl.ds((slot * nv + w) * ny, ny), :] = weight
            if slot == 1:
                total = total + weight * mixed(f_ref, w, lambda v: p0[v, edge])
    weight_ref[pl.ds(2 * nv * ny, ny), :] = total


def first_sweep(block, source, coef, metric, after):
    nv, nx, ny, nz = source.shape[1:]
    assert 2 < nx <= ROWS
    rows = (2 * nv + 1) * ny
    return call(
        first_kernel,
        "first_sweep",
        out_shape=(f32(nv, nx - 2, ny, nz), f32(nv, nx, ny, nz), f32(nx, nz), f32(rows, nz)),
        in_specs=[SMEM] + [VMEM] * 3 + [ANY],
        out_specs=(VMEM,) * 4,
        scratch_shapes=[
            pltpu.VMEM((nv, nx, ny, nz), jnp.float32),
            pltpu.VMEM((nv, ny, nz), jnp.float32),
            pltpu.VMEM((nx, ny, nz), jnp.float32),
        ],
    )(block, source, coef, metric, after)


def second_kernel(f_ref, far0, far1, state0, state1, sums_ref, whole0, whole1):
    nv, ny, nz = far0.shape
    rows = nv * ny
    for far, state, whole in ((far0, state0, whole0), (far1, state1, whole1)):
        rho = state[pl.ds(rows, ny), :]
        for w in range(nv):
            mix = mixed(f_ref, w, lambda v: far[v])
            whole[pl.ds(w * ny, ny), :] = state[pl.ds(w * ny, ny), :] + rho * mix
    for k in range(nz // 128):
        whole0[pl.ds(rows, ROWS), pl.ds(k * 128, 128)] = sums_ref[...]


def second_states(block, far, states, sums):
    nv, ny, nz = far[0].shape
    rows = nv * ny
    return call(
        second_kernel,
        "second_states",
        out_shape=(f32(rows + ROWS, nz), f32(rows, nz)),
        in_specs=[SMEM] + [VMEM] * 5,
        out_specs=(VMEM,) * 2,
    )(block, *far, *states, sums)


def last_kernel(c_ref, inner_ref, whole0, whole1, b_ref, base_ref, out_ref, p1):
    nv, nx, ny, nz = b_ref.shape
    zero = jnp.zeros((ny, nz), jnp.float32)
    for slot, whole in ((0, whole0), (1, whole1)):
        for v in range(nv):
            p1[v, edge_of(slot, nx)] = whole[pl.ds(v * ny, ny), :]

    def state(v, x):
        return inner_ref[v, x - 1] if 0 < x < nx - 1 else p1[v, x]

    for x in range(nx):
        along = [zero, zero, zero]
        for v in range(nv):
            b = b_ref[v, x]
            p = state(v, x)
            beside = [state(v, at) for at in (x - 1, x + 1) if 0 <= at < nx]
            along[0] = along[0] + b * sum(beside[1:], beside[0])
            along[1] = along[1] + b * shift_sum(p, 0)
            along[2] = along[2] + b * shift_sum(p, 1)
        own = c_ref[0, 1, x] * along[0] + c_ref[0, 2, x] * along[1] + c_ref[0, 3, x] * along[2]
        out_ref[x : x + 1, :] = base_ref[x : x + 1, :] + jnp.sum(own, axis=0, keepdims=True)


def last_sweep(coef, inner, edges, b, base):
    return call(
        last_kernel,
        "last_sweep",
        out_shape=f32(*base.shape),
        in_specs=[VMEM] * 6,
        out_specs=VMEM,
        scratch_shapes=[pltpu.VMEM(b.shape, jnp.float32)],
    )(coef, inner, *edges, b, base)


def factors(nodes, cells, sums):
    raw = [math.sin(math.pi * (n + 0.5) / nodes) for n in range(nodes)]
    weight = [r / sum(raw) for r in raw]
    objective = [sums[n : n + 1, :] * (1.0 / cells) for n in range(nodes)]
    mean = sum(w * o for w, o in zip(weight, objective))
    variance = sum(w * (o - mean) ** 2 for w, o in zip(weight, objective))
    spread = jnp.sqrt(variance + 0.25)
    return [w * (1.0 + 2.0 * (o - mean) / spread) for w, o in zip(weight, objective)]


def node_kernel(parts, few, sens_ref, weight_ref, even_ref, odd_ref, *refs):
    sums, outs, acc = refs[:few], refs[few:-1], refs[-1]
    nx, nz = sens_ref.shape
    rows = even_ref.shape[0] - ROWS
    acc[...] = jnp.zeros_like(acc)
    acc[pl.ds(0, nx), :] = sens_ref[...]
    total = even_ref[pl.ds(rows, ROWS), pl.ds(0, 128)]
    for other in sums:
        total = total + other[...]
    for k in range(nz // 128):
        acc[pl.ds(ROWS, ROWS), pl.ds(k * 128, 128)] = total
    total = weight_ref[pl.ds(0, rows), :] * even_ref[pl.ds(0, rows), :]
    acc[pl.ds(edge_of(0, nx), 1), :] += jnp.sum(total, axis=0, keepdims=True)
    total = weight_ref[pl.ds(rows, odd_ref.shape[0]), :] * odd_ref[...]
    acc[pl.ds(edge_of(1, nx), 1), :] += jnp.sum(total, axis=0, keepdims=True)
    for part, out in enumerate(outs):
        out[...] = share(acc, parts, 0, 2 * ROWS, part)


def node_terms(parts, sens, weight, even, odd, sums):
    nx, nz = sens.shape
    return call(
        functools.partial(node_kernel, parts, len(sums)),
        "node_terms",
        out_shape=(f32(2 * ROWS, nz // parts),) * parts,
        in_specs=[VMEM] * (4 + len(sums)),
        out_specs=(VMEM,) * parts,
        scratch_shapes=[pltpu.VMEM((2 * ROWS, nz), jnp.float32)],
    )(sens, weight, even, odd, *sums)


def gradient_kernel(nodes, cells, *refs):
    terms, out_ref = refs[:-1], refs[-1]
    nx = out_ref.shape[0]
    factor = factors(nodes, cells, sum(term[pl.ds(ROWS, ROWS), pl.ds(0, 128)] for term in terms))
    node = lax.axis_index("node")
    total = jnp.zeros(out_ref.shape, jnp.float32)
    for part, term in enumerate(terms):
        whose = node if part == 0 else 1 - node
        scale = factor[0]
        for n in range(1, nodes):
            scale = jnp.where(whose == n, factor[n], scale)
        total = total + term[pl.ds(0, nx), :] * scale[:, :1]
    out_ref[...] = total


def gradient(nodes, cells, nx, terms):
    return call(
        functools.partial(gradient_kernel, nodes, cells),
        "gradient",
        out_shape=f32(nx, terms[0].shape[1]),
        in_specs=[VMEM] * len(terms),
        out_specs=VMEM,
    )(*terms)


def swap_pairs(value, slot, part=0):
    count, nodes = lax.axis_size("slab"), lax.axis_size("node")
    pairs = []
    for low in range(slot, count - 1, 2):
        pairs += [(low, low + 1), (low + 1, low)]
    if part == 0:
        return lax.ppermute(value, "slab", pairs)
    cross = [(n * count + a, (1 - n) * count + b) for n in range(nodes) for a, b in pairs]
    return lax.ppermute(value, ("node", "slab"), cross)


def from_partner(value, slab, node=0):
    count, nodes = lax.axis_size("slab"), lax.axis_size("node")
    pairs = [(n * count + i, (n ^ node) * count + (i ^ slab)) for n in range(nodes) for i in range(count)]
    return lax.ppermute(value, ("node", "slab"), pairs)


def other_core(value):
    return lax.ppermute(value, "node", [(0, 1), (1, 0)])


def after(value, *others):
    return lax.optimization_barrier((value, *others))[0]


def per_device(source, coef, block, metric, wall):
    nodes, slabs = lax.axis_size("node"), lax.axis_size("slab")
    nx = source.shape[2]
    cells = wall.shape[1] * slabs * wall.shape[2]
    parts = 2 if nodes == 2 else 1
    assert slabs & (slabs - 1) == 0 and slabs > 4
    *own, sums = edge_state(source, coef, wall)
    far = [swap_pairs(value, slot) for slot, value in enumerate(own)]
    inner, b, base, weight = first_sweep(block, source, coef, metric, sums)
    first, *bits, last = [1 << k for k in range(1, slabs.bit_length() - 1)]
    sums = after(sums + from_partner(sums, first), base)
    states = edge_states(block, source, coef, sums)
    for slab in bits:
        sums = sums + from_partner(sums, slab)
    odd = swap_pairs(after(states[1], sums), 1)
    if parts == 1:
        sums = lax.psum(sums, "node")
    edges = second_states(block, far, states, sums)
    even = swap_pairs(edges[0], 0)
    sums = after(sums, edges[0])
    sums = [sums] + [from_partner(sums, last ^ k) for k in (0, 1)]
    sens = last_sweep(coef, inner, edges, b, base)
    terms = list(node_terms(parts, sens, weight, even, odd, sums))
    if parts == 2:
        terms[1] = other_core(terms[1])
        return gradient(nodes, cells, nx, terms)
    total = lax.psum(gradient(nodes, cells, nx, terms), "node")
    width = total.shape[1] // nodes
    return lax.dynamic_slice_in_dim(total, lax.axis_index("node") * width, width, 1)


def solution(mesh):
    return jax.shard_map(
        per_device,
        mesh=mesh,
        in_specs=(
            P("node", None, "slab", None, None),
            P("node", None, "slab", None, None),
            P("node", None, None),
            P("node", None, "slab", None, None),
            P("node", "slab", None),
        ),
        out_specs=P("slab", "node"),
        check_vma=False,
    )
```

```python
import functools
import math

import jax
import jax.numpy as jnp
from jax import lax
from jax.experimental import pallas as pl
from jax.experimental.pallas import tpu as pltpu
from jax.sharding import PartitionSpec as P

ROWS = 8
COST = {"last_sweep": 1}
LIMIT = {"edge_state": 62}


def call(kernel, name, **kw):
    us, limit = COST.get(name, 0), LIMIT.get(name, 24)
    return pl.pallas_call(
        kernel,
        compiler_params=pltpu.CompilerParams(vmem_limit_bytes=limit * 1024 * 1024),
        cost_estimate=pl.CostEstimate(flops=int(us * 1.1e9), bytes_accessed=0, transcendentals=0),
        name=name,
        **kw,
    )


def f32(*shape):
    return jax.ShapeDtypeStruct(shape, jnp.float32)


VMEM = pl.BlockSpec(memory_space=pltpu.VMEM)
SMEM = pl.BlockSpec(memory_space=pltpu.SMEM)
ANY = pl.BlockSpec(memory_space=pl.ANY)


def edge_of(slot, planes):
    up = lax.rem(lax.axis_index("slab") + slot, 2) == 0
    return jnp.where(up, planes - 1, 0)


def inverse_diag(c):
    return 1.0 / (0.5 + c(0) + 2.4 * (c(1) + c(2) + c(3)))


def shift_sum(p, axis):
    size = p.shape[axis]
    place = lax.broadcasted_iota(jnp.int32, p.shape, axis)
    ahead = jnp.where(place < size - 1, pltpu.roll(p, size - 1, axis), 0.0)
    behind = jnp.where(place > 0, pltpu.roll(p, 1, axis), 0.0)
    return ahead + behind


def edge_kernel(
    s_ref, c_ref, wall_ref, u0, u1, wsum_ref, s_buf, c_buf, wall_buf, c_sems, s_sems, wall_sem
):
    nv, nx = s_ref.shape[1:3]
    edges = [edge_of(slot, nx) for slot in (0, 1)]
    c_copies = [pltpu.make_async_copy(c_ref.at[0, :, e], c_buf.at[j], c_sems.at[j]) for j, e in enumerate(edges)]
    s_copies = [pltpu.make_async_copy(s_ref.at[0, :, e], s_buf.at[j], s_sems.at[j]) for j, e in enumerate(edges)]
    wall_copy = pltpu.make_async_copy(wall_ref.at[0], wall_buf, wall_sem)
    for j in (0, 1):
        c_copies[j].start()
        s_copies[j].start()
    wall_copy.start()
    for j, u in enumerate((u0, u1)):
        c_copies[j].wait()
        inv = inverse_diag(lambda k: c_buf[j, k])
        s_copies[j].wait()
        for v in range(nv):
            u[v] = s_buf[j, v] * inv
    wall_copy.wait()
    wall = jnp.sum(jnp.sum(wall_buf[...], axis=0, keepdims=True), axis=1, keepdims=True)
    rows = lax.broadcasted_iota(jnp.int32, wsum_ref.shape, 0)
    wsum_ref[...] = jnp.where(rows == lax.axis_index("node"), wall, 0.0)


def edge_state(source, coef, wall):
    nv, ny, nz = source.shape[1], source.shape[3], source.shape[4]
    return call(
        edge_kernel,
        "edge_state",
        out_shape=(f32(nv, ny, nz),) * 2 + (f32(ROWS, 128),),
        in_specs=[ANY] * 3,
        out_specs=(VMEM,) * 3,
        scratch_shapes=[
            pltpu.VMEM((2, nv, ny, nz), jnp.float32),
            pltpu.VMEM((2, 4, ny, nz), jnp.float32),
            pltpu.VMEM(wall.shape[1:], jnp.float32),
            pltpu.SemaphoreType.DMA((2,)),
            pltpu.SemaphoreType.DMA((2,)),
            pltpu.SemaphoreType.DMA,
        ],
    )(source, coef, wall)


def share(buf, parts, first, rows, part):
    width = buf.shape[1] // parts
    if parts == 1:
        return buf[pl.ds(first, rows), :]
    node = lax.axis_index("node")
    at = pl.multiple_of((node if part == 0 else 1 - node) * width, width)
    return buf[pl.ds(first, rows), pl.ds(at, width)]


def coupled(c_ref, x, below, here, above):
    q = c_ref[0, 1, x] * (below + above)
    q = q + c_ref[0, 2, x] * shift_sum(here, 0)
    return q + c_ref[0, 3, x] * shift_sum(here, 1)


def mixed(f_ref, w, q):
    mix = f_ref[0, 0, w] * q(0)
    for v in range(1, f_ref.shape[1]):
        mix = mix + f_ref[0, v, w] * q(v)
    return mix


def state_kernel(slot, f_ref, s_ref, c_ref, after, out, q_ref, p_ref):
    del after
    nv, nx, ny, nz = s_ref.shape[1:]
    zero = jnp.zeros((ny, nz), jnp.float32)
    edge = edge_of(slot, nx)
    inner = jnp.where(edge == 0, 1, nx - 2)
    inv = inverse_diag(lambda k: c_ref[0, k, edge])
    inv_inner = inverse_diag(lambda k: c_ref[0, k, inner])
    for v in range(nv):
        p_ref[v] = s_ref[0, v, edge] * inv
        beside = s_ref[0, v, inner] * inv_inner
        q_ref[v] = coupled(c_ref, edge, beside, p_ref[v], zero)
    for w in range(nv):
        out[pl.ds(w * ny, ny), :] = p_ref[w] + inv * mixed(f_ref, w, lambda v: q_ref[v])
    out[pl.ds(nv * ny, ny), :] = c_ref[0, 1, edge] * inv


def edge_second(slot, block, source, coef, after):
    nv, nx, ny, nz = source.shape[1:]
    return call(
        functools.partial(state_kernel, slot),
        f"edge_second{slot}",
        out_shape=f32((nv + 1) * ny, nz),
        in_specs=[SMEM] + [VMEM] * 2 + [ANY],
        out_specs=VMEM,
        scratch_shapes=[pltpu.VMEM((nv, ny, nz), jnp.float32)] * 2,
    )(block, source, coef, after)


def first_kernel(parts, f_ref, s_ref, c_ref, m_ref, after, p1_ref, b_ref, sens_ref, weight_ref, *refs):
    del after
    shares, (p0, q_ref, inv_ref) = refs[:parts], refs[parts:]
    nv, nx, ny, nz = s_ref.shape[1:]

    def start(x, _):
        inv = inverse_diag(lambda k: c_ref[0, k, x])
        inv_ref[x] = inv
        own = jnp.zeros((ny, nz), jnp.float32)
        for v in range(nv):
            p = s_ref[0, v, x] * inv
            p0[v, x] = p
            own = own + m_ref[0, v, x] * p
            q_ref[v] = m_ref[0, v, x] * inv
        sens_ref[pl.ds(x, 1), :] = jnp.sum(own, axis=0, keepdims=True)
        for v in range(nv):
            b = f_ref[0, v, 0] * q_ref[0]
            for w in range(1, nv):
                b = b + f_ref[0, v, w] * q_ref[w]
            b_ref[v, x] = b
        return 0

    lax.fori_loop(0, nx, start, 0)

    def first(x, _):
        for v in range(nv):
            q_ref[v] = coupled(c_ref, x, p0[v, x - 1], p0[v, x], p0[v, x + 1])
        for w in range(nv):
            p1_ref[w, x - 1] = p0[w, x] + inv_ref[x] * mixed(f_ref, w, lambda v: q_ref[v])
        return 0

    lax.fori_loop(1, nx - 1, first, 0)

    for slot in (0, 1):
        edge = edge_of(slot, nx)
        total = jnp.zeros((ny, nz), jnp.float32)
        for w in range(nv):
            weight = c_ref[0, 1, edge] * b_ref[w, edge]
            weight_ref[pl.ds((slot * nv + w) * ny, ny), :] = weight
            if slot == 1:
                total = total + weight * mixed(f_ref, w, lambda v: p0[v, edge])
    weight_ref[pl.ds(2 * nv * ny, ny), :] = total
    for part, out in enumerate(shares):
        out[...] = share(weight_ref, parts, 0, nv * ny, part)


def first_sweep(parts, block, source, coef, metric, after):
    nv, nx, ny, nz = source.shape[1:]
    assert 2 < nx <= ROWS
    rows = (2 * nv + 1) * ny
    return call(
        functools.partial(first_kernel, parts),
        "first_sweep",
        out_shape=(f32(nv, nx - 2, ny, nz), f32(nv, nx, ny, nz), f32(nx, nz), f32(rows, nz))
        + (f32(nv * ny, nz // parts),) * parts,
        in_specs=[SMEM] + [VMEM] * 3 + [ANY],
        out_specs=(VMEM,) * (4 + parts),
        scratch_shapes=[
            pltpu.VMEM((nv, nx, ny, nz), jnp.float32),
            pltpu.VMEM((nv, ny, nz), jnp.float32),
            pltpu.VMEM((nx, ny, nz), jnp.float32),
        ],
    )(block, source, coef, metric, after)


def second_kernel(parts, f_ref, far0, far1, state0, state1, sums_ref, whole0, whole1, *msgs):
    nv, ny, nz = far0.shape
    rows = nv * ny
    for far, state, whole in ((far0, state0, whole0), (far1, state1, whole1)):
        rho = state[pl.ds(rows, ny), :]
        for w in range(nv):
            mix = mixed(f_ref, w, lambda v: far[v])
            whole[pl.ds(w * ny, ny), :] = state[pl.ds(w * ny, ny), :] + rho * mix
    for part, msg in enumerate(msgs):
        msg[pl.ds(0, rows), :] = share(whole0, parts, 0, rows, part)
        for k in range(msg.shape[1] // 128):
            msg[pl.ds(rows, ROWS), pl.ds(k * 128, 128)] = sums_ref[...]


def second_states(parts, block, far, states, sums):
    nv, ny, nz = far[0].shape
    return call(
        functools.partial(second_kernel, parts),
        "second_states",
        out_shape=(f32(nv * ny, nz),) * 2 + (f32(nv * ny + ROWS, nz // parts),) * parts,
        in_specs=[SMEM] + [VMEM] * 5,
        out_specs=(VMEM,) * (2 + parts),
    )(block, *far, *states, sums)


def last_kernel(c_ref, inner_ref, whole0, whole1, b_ref, base_ref, out_ref, p1):
    nv, nx, ny, nz = b_ref.shape
    zero = jnp.zeros((ny, nz), jnp.float32)
    for slot, whole in ((0, whole0), (1, whole1)):
        for v in range(nv):
            p1[v, edge_of(slot, nx)] = whole[pl.ds(v * ny, ny), :]

    def state(v, x):
        return inner_ref[v, x - 1] if 0 < x < nx - 1 else p1[v, x]

    for x in range(nx):
        along = [zero, zero, zero]
        for v in range(nv):
            b = b_ref[v, x]
            p = state(v, x)
            beside = [state(v, at) for at in (x - 1, x + 1) if 0 <= at < nx]
            along[0] = along[0] + b * sum(beside[1:], beside[0])
            along[1] = along[1] + b * shift_sum(p, 0)
            along[2] = along[2] + b * shift_sum(p, 1)
        own = c_ref[0, 1, x] * along[0] + c_ref[0, 2, x] * along[1] + c_ref[0, 3, x] * along[2]
        out_ref[x : x + 1, :] = base_ref[x : x + 1, :] + jnp.sum(own, axis=0, keepdims=True)


def last_sweep(coef, inner, edges, b, base):
    return call(
        last_kernel,
        "last_sweep",
        out_shape=f32(*base.shape),
        in_specs=[VMEM] * 6,
        out_specs=VMEM,
        scratch_shapes=[pltpu.VMEM(b.shape, jnp.float32)],
    )(coef, inner, *edges, b, base)


def factors(nodes, cells, sums):
    raw = [math.sin(math.pi * (n + 0.5) / nodes) for n in range(nodes)]
    weight = [r / sum(raw) for r in raw]
    objective = [sums[n : n + 1, :] * (1.0 / cells) for n in range(nodes)]
    mean = sum(w * o for w, o in zip(weight, objective))
    variance = sum(w * (o - mean) ** 2 for w, o in zip(weight, objective))
    spread = jnp.sqrt(variance + 0.25)
    return [w * (1.0 + 2.0 * (o - mean) / spread) for w, o in zip(weight, objective)]


def node_kernel(parts, few, sens_ref, weight_ref, odd_ref, *refs):
    sums, outs, acc = refs[:few], refs[few + 1 : -1], refs[-1]
    nx, nz = sens_ref.shape
    rows = odd_ref.shape[0]
    acc[...] = jnp.zeros_like(acc)
    acc[pl.ds(0, nx), :] = sens_ref[...]
    total = sums[0][...]
    for other in sums[1:]:
        total = total + other[...]
    for k in range(nz // 128):
        acc[pl.ds(ROWS, ROWS), pl.ds(k * 128, 128)] = total
    total = weight_ref[pl.ds(weight_ref.shape[0] - rows, rows), :] * odd_ref[...]
    acc[pl.ds(edge_of(1, nx), 1), :] += jnp.sum(total, axis=0, keepdims=True)
    for part, out in enumerate(outs):
        out[...] = share(acc, parts, 0, 2 * ROWS, part)


def node_terms(parts, sens, weight, odd, sums, after):
    nx, nz = sens.shape
    return call(
        functools.partial(node_kernel, parts, len(sums)),
        "node_terms",
        out_shape=(f32(2 * ROWS, nz // parts),) * parts,
        in_specs=[VMEM] * (3 + len(sums)) + [ANY],
        out_specs=(VMEM,) * parts,
        scratch_shapes=[pltpu.VMEM((2 * ROWS, nz), jnp.float32)],
    )(sens, weight, odd, *sums, after)


def gradient_kernel(parts, nodes, cells, *refs):
    terms, weights, msgs = (refs[k * parts : (k + 1) * parts] for k in range(3))
    out_ref, acc = refs[3 * parts :]
    nx = out_ref.shape[0]
    rows = weights[0].shape[0]
    sums = sum(r[pl.ds(at, ROWS), pl.ds(0, 128)] for refs, at in ((terms, ROWS), (msgs, rows)) for r in refs)
    factor = factors(nodes, cells, sums)
    node = lax.axis_index("node")
    out_ref[...] = jnp.zeros_like(out_ref)
    for part in range(parts):
        acc[...] = terms[part][pl.ds(0, ROWS), :]
        total = weights[part][...] * msgs[part][pl.ds(0, rows), :]
        acc[pl.ds(edge_of(0, nx), 1), :] += jnp.sum(total, axis=0, keepdims=True)
        whose = node if part == 0 else 1 - node
        scale = factor[0]
        for n in range(1, nodes):
            scale = jnp.where(whose == n, factor[n], scale)
        out_ref[...] += acc[pl.ds(0, nx), :] * scale[:, :1]


def gradient(nodes, cells, nx, terms, weights, msgs):
    parts, width = len(terms), terms[0].shape[1]
    return call(
        functools.partial(gradient_kernel, parts, nodes, cells),
        "gradient",
        out_shape=f32(nx, width),
        in_specs=[VMEM] * (3 * parts),
        out_specs=VMEM,
        scratch_shapes=[pltpu.VMEM((ROWS, width), jnp.float32)],
    )(*terms, *weights, *msgs)


def swap_pairs(value, slot, part=0):
    count, nodes = lax.axis_size("slab"), lax.axis_size("node")
    pairs = []
    for low in range(slot, count - 1, 2):
        pairs += [(low, low + 1), (low + 1, low)]
    if part == 0:
        return lax.ppermute(value, "slab", pairs)
    cross = [(n * count + a, (1 - n) * count + b) for n in range(nodes) for a, b in pairs]
    return lax.ppermute(value, ("node", "slab"), cross)


def from_partner(value, slab, node=0):
    count, nodes = lax.axis_size("slab"), lax.axis_size("node")
    pairs = [(n * count + i, (n ^ node) * count + (i ^ slab)) for n in range(nodes) for i in range(count)]
    return lax.ppermute(value, ("node", "slab"), pairs)


def other_core(value):
    return lax.ppermute(value, "node", [(0, 1), (1, 0)])


def after(value, *others):
    return lax.optimization_barrier((value, *others))[0]


def per_device(source, coef, block, metric, wall):
    nodes, slabs = lax.axis_size("node"), lax.axis_size("slab")
    nx = source.shape[2]
    cells = wall.shape[1] * slabs * wall.shape[2]
    parts = 2 if nodes == 2 else 1
    assert slabs & (slabs - 1) == 0 and slabs > 4
    *own, sums = edge_state(source, coef, wall)
    far = [swap_pairs(value, slot) for slot, value in enumerate(own)]
    inner, b, base, weight, *weights = first_sweep(parts, block, source, coef, metric, sums)
    first, *bits = [1 << k for k in range(1, slabs.bit_length() - 1)]
    sums = after(sums + from_partner(sums, first), base)
    states = [edge_second(0, block, source, coef, sums)]
    for slab in bits[:-1]:
        sums = sums + from_partner(sums, slab)
    if parts == 1:
        sums = lax.psum(sums, "node")
    states.append(edge_second(1, block, source, coef, sums))
    odd = swap_pairs(states[1], 1)
    edges = second_states(parts, block, far, states, sums)
    evens = [swap_pairs(value, 0, part) for part, value in enumerate(edges[2:])]
    sums = after(sums, edges[0])
    sums = [sums] + [from_partner(sums, bits[-1] ^ k) for k in (0, 1)]
    weights[1:] = [other_core(value) for value in weights[1:]]
    sens = last_sweep(coef, inner, edges[:2], b, base)
    terms = list(node_terms(parts, sens, weight, odd, sums, weights[-1]))
    terms[1:] = [other_core(value) for value in terms[1:]]
    term = gradient(nodes, cells, nx, terms, weights, evens)
    if parts == 2:
        return term
    total = lax.psum(term, "node")
    width = total.shape[1] // nodes
    return lax.dynamic_slice_in_dim(total, lax.axis_index("node") * width, width, 1)


def solution(mesh):
    return jax.shard_map(
        per_device,
        mesh=mesh,
        in_specs=(
            P("node", None, "slab", None, None),
            P("node", None, "slab", None, None),
            P("node", None, None),
            P("node", None, "slab", None, None),
            P("node", "slab", None),
        ),
        out_specs=P("slab", "node"),
        check_vma=False,
    )
```

```python
import functools
import math

import jax
import jax.numpy as jnp
from jax import lax
from jax.experimental import pallas as pl
from jax.experimental.pallas import tpu as pltpu
from jax.sharding import PartitionSpec as P

ROWS = 8
COST = {"last_sweep": 1}
LIMIT = {"edge_state": 62}


def call(kernel, name, **kw):
    us, limit = COST.get(name, 0), LIMIT.get(name, 24)
    return pl.pallas_call(
        kernel,
        compiler_params=pltpu.CompilerParams(vmem_limit_bytes=limit * 1024 * 1024),
        cost_estimate=pl.CostEstimate(flops=int(us * 1.1e9), bytes_accessed=0, transcendentals=0),
        name=name,
        **kw,
    )


def f32(*shape):
    return jax.ShapeDtypeStruct(shape, jnp.float32)


VMEM = pl.BlockSpec(memory_space=pltpu.VMEM)
SMEM = pl.BlockSpec(memory_space=pltpu.SMEM)
ANY = pl.BlockSpec(memory_space=pl.ANY)


def edge_of(slot, planes):
    up = lax.rem(lax.axis_index("slab") + slot, 2) == 0
    return jnp.where(up, planes - 1, 0)


def inverse_diag(c):
    return 1.0 / (0.5 + c(0) + 2.4 * (c(1) + c(2) + c(3)))


def shift_sum(p, axis):
    size = p.shape[axis]
    place = lax.broadcasted_iota(jnp.int32, p.shape, axis)
    ahead = jnp.where(place < size - 1, pltpu.roll(p, size - 1, axis), 0.0)
    behind = jnp.where(place > 0, pltpu.roll(p, 1, axis), 0.0)
    return ahead + behind


def edge_kernel(
    s_ref, c_ref, wall_ref, u0, u1, wsum_ref, s_buf, c_buf, wall_buf, c_sems, s_sems, wall_sem
):
    nv, nx = s_ref.shape[1:3]
    edges = [edge_of(slot, nx) for slot in (0, 1)]
    c_copies = [pltpu.make_async_copy(c_ref.at[0, :, e], c_buf.at[j], c_sems.at[j]) for j, e in enumerate(edges)]
    s_copies = [pltpu.make_async_copy(s_ref.at[0, :, e], s_buf.at[j], s_sems.at[j]) for j, e in enumerate(edges)]
    wall_copy = pltpu.make_async_copy(wall_ref.at[0], wall_buf, wall_sem)
    for j in (0, 1):
        c_copies[j].start()
        s_copies[j].start()
    wall_copy.start()
    for j, u in enumerate((u0, u1)):
        c_copies[j].wait()
        inv = inverse_diag(lambda k: c_buf[j, k])
        s_copies[j].wait()
        for v in range(nv):
            u[v] = s_buf[j, v] * inv
    wall_copy.wait()
    wall = jnp.sum(jnp.sum(wall_buf[...], axis=0, keepdims=True), axis=1, keepdims=True)
    rows = lax.broadcasted_iota(jnp.int32, wsum_ref.shape, 0)
    wsum_ref[...] = jnp.where(rows == lax.axis_index("node"), wall, 0.0)


def edge_state(source, coef, wall):
    nv, ny, nz = source.shape[1], source.shape[3], source.shape[4]
    return call(
        edge_kernel,
        "edge_state",
        out_shape=(f32(nv, ny, nz),) * 2 + (f32(ROWS, 128),),
        in_specs=[ANY] * 3,
        out_specs=(VMEM,) * 3,
        scratch_shapes=[
            pltpu.VMEM((2, nv, ny, nz), jnp.float32),
            pltpu.VMEM((2, 4, ny, nz), jnp.float32),
            pltpu.VMEM(wall.shape[1:], jnp.float32),
            pltpu.SemaphoreType.DMA((2,)),
            pltpu.SemaphoreType.DMA((2,)),
            pltpu.SemaphoreType.DMA,
        ],
    )(source, coef, wall)


def share(buf, parts, first, rows, part):
    width = buf.shape[1] // parts
    if parts == 1:
        return buf[pl.ds(first, rows), :]
    node = lax.axis_index("node")
    at = pl.multiple_of((node if part == 0 else 1 - node) * width, width)
    return buf[pl.ds(first, rows), pl.ds(at, width)]


def coupled(c_ref, x, below, here, above):
    q = c_ref[0, 1, x] * (below + above)
    q = q + c_ref[0, 2, x] * shift_sum(here, 0)
    return q + c_ref[0, 3, x] * shift_sum(here, 1)


def mixed(f_ref, w, q):
    mix = f_ref[0, 0, w] * q(0)
    for v in range(1, f_ref.shape[1]):
        mix = mix + f_ref[0, v, w] * q(v)
    return mix


def state_kernel(slot, f_ref, s_ref, c_ref, after, out, q_ref, p_ref):
    del after
    nv, nx, ny, nz = s_ref.shape[1:]
    zero = jnp.zeros((ny, nz), jnp.float32)
    edge = edge_of(slot, nx)
    inner = jnp.where(edge == 0, 1, nx - 2)
    inv = inverse_diag(lambda k: c_ref[0, k, edge])
    inv_inner = inverse_diag(lambda k: c_ref[0, k, inner])
    for v in range(nv):
        p_ref[v] = s_ref[0, v, edge] * inv
        beside = s_ref[0, v, inner] * inv_inner
        q_ref[v] = coupled(c_ref, edge, beside, p_ref[v], zero)
    for w in range(nv):
        out[pl.ds(w * ny, ny), :] = p_ref[w] + inv * mixed(f_ref, w, lambda v: q_ref[v])
    out[pl.ds(nv * ny, ny), :] = c_ref[0, 1, edge] * inv


def edge_second(slot, block, source, coef, after):
    nv, nx, ny, nz = source.shape[1:]
    return call(
        functools.partial(state_kernel, slot),
        f"edge_second{slot}",
        out_shape=f32((nv + 1) * ny, nz),
        in_specs=[SMEM] + [VMEM] * 2 + [ANY],
        out_specs=VMEM,
        scratch_shapes=[pltpu.VMEM((nv, ny, nz), jnp.float32)] * 2,
    )(block, source, coef, after)


def first_kernel(f_ref, s_ref, c_ref, m_ref, after, p1_ref, b_ref, sens_ref, p0, q_ref, inv_ref):
    del after
    nv, nx, ny, nz = s_ref.shape[1:]

    def start(x, _):
        inv = inverse_diag(lambda k: c_ref[0, k, x])
        inv_ref[x] = inv
        own = jnp.zeros((ny, nz), jnp.float32)
        for v in range(nv):
            p = s_ref[0, v, x] * inv
            p0[v, x] = p
            own = own + m_ref[0, v, x] * p
            q_ref[v] = m_ref[0, v, x] * inv
        sens_ref[pl.ds(x, 1), :] = jnp.sum(own, axis=0, keepdims=True)
        for v in range(nv):
            b = f_ref[0, v, 0] * q_ref[0]
            for w in range(1, nv):
                b = b + f_ref[0, v, w] * q_ref[w]
            b_ref[v, x] = b
        return 0

    lax.fori_loop(0, nx, start, 0)

    def first(x, _):
        for v in range(nv):
            q_ref[v] = coupled(c_ref, x, p0[v, x - 1], p0[v, x], p0[v, x + 1])
        for w in range(nv):
            p1_ref[w, x - 1] = p0[w, x] + inv_ref[x] * mixed(f_ref, w, lambda v: q_ref[v])
        return 0

    lax.fori_loop(1, nx - 1, first, 0)


def first_sweep(block, source, coef, metric, after):
    nv, nx, ny, nz = source.shape[1:]
    assert 2 < nx <= ROWS
    return call(
        first_kernel,
        "first_sweep",
        out_shape=(f32(nv, nx - 2, ny, nz), f32(nv, nx, ny, nz), f32(nx, nz)),
        in_specs=[SMEM] + [VMEM] * 3 + [ANY],
        out_specs=(VMEM,) * 3,
        scratch_shapes=[
            pltpu.VMEM((nv, nx, ny, nz), jnp.float32),
            pltpu.VMEM((nv, ny, nz), jnp.float32),
            pltpu.VMEM((nx, ny, nz), jnp.float32),
        ],
    )(block, source, coef, metric, after)


def weights_kernel(parts, f_ref, c_ref, b_ref, own_ref, after, weight_ref, *shares):
    del after
    nv, nx, ny, nz = b_ref.shape
    total = jnp.zeros((ny, nz), jnp.float32)
    for slot in (0, 1):
        edge = edge_of(slot, nx)
        for w in range(nv):
            weight = c_ref[0, 1, edge] * b_ref[w, edge]
            weight_ref[pl.ds((slot * nv + w) * ny, ny), :] = weight
            if slot == 1:
                total = total + weight * mixed(f_ref, w, lambda v: own_ref[v])
    weight_ref[pl.ds(2 * nv * ny, ny), :] = total
    for part, out in enumerate(shares):
        out[...] = share(weight_ref, parts, 0, nv * ny, part)


def edge_weights(parts, block, coef, b, own, after):
    nv, nx, ny, nz = b.shape
    rows = (2 * nv + 1) * ny
    return call(
        functools.partial(weights_kernel, parts),
        "edge_weights",
        out_shape=(f32(rows, nz),) + (f32(nv * ny, nz // parts),) * parts,
        in_specs=[SMEM] + [VMEM] * 3 + [ANY],
        out_specs=(VMEM,) * (1 + parts),
    )(block, coef, b, own, after)


def second_kernel(parts, f_ref, far0, far1, state0, state1, sums_ref, whole0, whole1, *msgs):
    nv, ny, nz = far0.shape
    rows = nv * ny
    for far, state, whole in ((far0, state0, whole0), (far1, state1, whole1)):
        rho = state[pl.ds(rows, ny), :]
        for w in range(nv):
            mix = mixed(f_ref, w, lambda v: far[v])
            whole[pl.ds(w * ny, ny), :] = state[pl.ds(w * ny, ny), :] + rho * mix
    for part, msg in enumerate(msgs):
        msg[pl.ds(0, rows), :] = share(whole0, parts, 0, rows, part)
        for k in range(msg.shape[1] // 128):
            msg[pl.ds(rows, ROWS), pl.ds(k * 128, 128)] = sums_ref[...]


def second_states(parts, block, far, states, sums):
    nv, ny, nz = far[0].shape
    return call(
        functools.partial(second_kernel, parts),
        "second_states",
        out_shape=(f32(nv * ny, nz),) * 2 + (f32(nv * ny + ROWS, nz // parts),) * parts,
        in_specs=[SMEM] + [VMEM] * 5,
        out_specs=(VMEM,) * (2 + parts),
    )(block, *far, *states, sums)


def last_kernel(c_ref, inner_ref, whole0, whole1, b_ref, base_ref, out_ref, p1):
    nv, nx, ny, nz = b_ref.shape
    zero = jnp.zeros((ny, nz), jnp.float32)
    for slot, whole in ((0, whole0), (1, whole1)):
        for v in range(nv):
            p1[v, edge_of(slot, nx)] = whole[pl.ds(v * ny, ny), :]

    def state(v, x):
        return inner_ref[v, x - 1] if 0 < x < nx - 1 else p1[v, x]

    for x in range(nx):
        along = [zero, zero, zero]
        for v in range(nv):
            b = b_ref[v, x]
            p = state(v, x)
            beside = [state(v, at) for at in (x - 1, x + 1) if 0 <= at < nx]
            along[0] = along[0] + b * sum(beside[1:], beside[0])
            along[1] = along[1] + b * shift_sum(p, 0)
            along[2] = along[2] + b * shift_sum(p, 1)
        own = c_ref[0, 1, x] * along[0] + c_ref[0, 2, x] * along[1] + c_ref[0, 3, x] * along[2]
        out_ref[x : x + 1, :] = base_ref[x : x + 1, :] + jnp.sum(own, axis=0, keepdims=True)


def last_sweep(coef, inner, edges, b, base):
    return call(
        last_kernel,
        "last_sweep",
        out_shape=f32(*base.shape),
        in_specs=[VMEM] * 6,
        out_specs=VMEM,
        scratch_shapes=[pltpu.VMEM(b.shape, jnp.float32)],
    )(coef, inner, *edges, b, base)


def factors(nodes, cells, sums):
    raw = [math.sin(math.pi * (n + 0.5) / nodes) for n in range(nodes)]
    weight = [r / sum(raw) for r in raw]
    objective = [sums[n : n + 1, :] * (1.0 / cells) for n in range(nodes)]
    mean = sum(w * o for w, o in zip(weight, objective))
    variance = sum(w * (o - mean) ** 2 for w, o in zip(weight, objective))
    spread = jnp.sqrt(variance + 0.25)
    return [w * (1.0 + 2.0 * (o - mean) / spread) for w, o in zip(weight, objective)]


def node_kernel(parts, few, sens_ref, weight_ref, odd_ref, *refs):
    sums, outs, acc = refs[:few], refs[few + 1 : -1], refs[-1]
    nx, nz = sens_ref.shape
    rows = odd_ref.shape[0]
    acc[...] = jnp.zeros_like(acc)
    acc[pl.ds(0, nx), :] = sens_ref[...]
    total = sums[0][...]
    for other in sums[1:]:
        total = total + other[...]
    for k in range(nz // 128):
        acc[pl.ds(ROWS, ROWS), pl.ds(k * 128, 128)] = total
    total = weight_ref[pl.ds(weight_ref.shape[0] - rows, rows), :] * odd_ref[...]
    acc[pl.ds(edge_of(1, nx), 1), :] += jnp.sum(total, axis=0, keepdims=True)
    for part, out in enumerate(outs):
        out[...] = share(acc, parts, 0, 2 * ROWS, part)


def node_terms(parts, sens, weight, odd, sums, after):
    nx, nz = sens.shape
    return call(
        functools.partial(node_kernel, parts, len(sums)),
        "node_terms",
        out_shape=(f32(2 * ROWS, nz // parts),) * parts,
        in_specs=[VMEM] * (3 + len(sums)) + [ANY],
        out_specs=(VMEM,) * parts,
        scratch_shapes=[pltpu.VMEM((2 * ROWS, nz), jnp.float32)],
    )(sens, weight, odd, *sums, after)


def gradient_kernel(parts, nodes, cells, *refs):
    terms, weights, msgs = (refs[k * parts : (k + 1) * parts] for k in range(3))
    out_ref, acc = refs[3 * parts :]
    nx = out_ref.shape[0]
    rows = weights[0].shape[0]
    sums = sum(r[pl.ds(at, ROWS), pl.ds(0, 128)] for refs, at in ((terms, ROWS), (msgs, rows)) for r in refs)
    factor = factors(nodes, cells, sums)
    node = lax.axis_index("node")
    out_ref[...] = jnp.zeros_like(out_ref)
    for part in range(parts):
        acc[...] = terms[part][pl.ds(0, ROWS), :]
        total = weights[part][...] * msgs[part][pl.ds(0, rows), :]
        acc[pl.ds(edge_of(0, nx), 1), :] += jnp.sum(total, axis=0, keepdims=True)
        whose = node if part == 0 else 1 - node
        scale = factor[0]
        for n in range(1, nodes):
            scale = jnp.where(whose == n, factor[n], scale)
        out_ref[...] += acc[pl.ds(0, nx), :] * scale[:, :1]


def gradient(nodes, cells, nx, terms, weights, msgs):
    parts, width = len(terms), terms[0].shape[1]
    return call(
        functools.partial(gradient_kernel, parts, nodes, cells),
        "gradient",
        out_shape=f32(nx, width),
        in_specs=[VMEM] * (3 * parts),
        out_specs=VMEM,
        scratch_shapes=[pltpu.VMEM((ROWS, width), jnp.float32)],
    )(*terms, *weights, *msgs)


def swap_pairs(value, slot, part=0):
    count, nodes = lax.axis_size("slab"), lax.axis_size("node")
    pairs = []
    for low in range(slot, count - 1, 2):
        pairs += [(low, low + 1), (low + 1, low)]
    if part == 0:
        return lax.ppermute(value, "slab", pairs)
    cross = [(n * count + a, (1 - n) * count + b) for n in range(nodes) for a, b in pairs]
    return lax.ppermute(value, ("node", "slab"), cross)


def from_partner(value, slab, node=0):
    count, nodes = lax.axis_size("slab"), lax.axis_size("node")
    pairs = [(n * count + i, (n ^ node) * count + (i ^ slab)) for n in range(nodes) for i in range(count)]
    return lax.ppermute(value, ("node", "slab"), pairs)


def other_core(value):
    return lax.ppermute(value, "node", [(0, 1), (1, 0)])


def after(value, *others):
    return lax.optimization_barrier((value, *others))[0]


def per_device(source, coef, block, metric, wall):
    nodes, slabs = lax.axis_size("node"), lax.axis_size("slab")
    nx = source.shape[2]
    cells = wall.shape[1] * slabs * wall.shape[2]
    parts = 2 if nodes == 2 else 1
    assert slabs & (slabs - 1) == 0 and slabs > 4
    *own, sums = edge_state(source, coef, wall)
    far = [swap_pairs(value, slot) for slot, value in enumerate(own)]
    inner, b, base = first_sweep(block, source, coef, metric, sums)
    first, *bits = [1 << k for k in range(1, slabs.bit_length() - 1)]
    sums = after(sums + from_partner(sums, first), base)
    states = [edge_second(0, block, source, coef, sums)]
    for slab in bits[:-1]:
        sums = sums + from_partner(sums, slab)
    if parts == 1:
        sums = lax.psum(sums, "node")
    states.append(edge_second(1, block, source, coef, after(sums, states[0])))
    odd = swap_pairs(states[1], 1)
    edges = second_states(parts, block, far, states, sums)
    evens = [swap_pairs(value, 0, part) for part, value in enumerate(edges[2:])]
    sums = after(sums, edges[0])
    sums = [sums] + [from_partner(sums, bits[-1] ^ k) for k in (0, 1)]
    weight, *weights = edge_weights(parts, block, coef, b, own[1], states[1])
    weights[1:] = [other_core(value) for value in weights[1:]]
    sens = last_sweep(coef, inner, edges[:2], b, base)
    terms = list(node_terms(parts, sens, weight, odd, sums, weights[-1]))
    terms[1:] = [other_core(value) for value in terms[1:]]
    term = gradient(nodes, cells, nx, terms, weights, evens)
    if parts == 2:
        return term
    total = lax.psum(term, "node")
    width = total.shape[1] // nodes
    return lax.dynamic_slice_in_dim(total, lax.axis_index("node") * width, width, 1)


def solution(mesh):
    return jax.shard_map(
        per_device,
        mesh=mesh,
        in_specs=(
            P("node", None, "slab", None, None),
            P("node", None, "slab", None, None),
            P("node", None, None),
            P("node", None, "slab", None, None),
            P("node", "slab", None),
        ),
        out_specs=P("slab", "node"),
        check_vma=False,
    )
```

```python
import functools
import math

import jax
import jax.numpy as jnp
from jax import lax
from jax.experimental import pallas as pl
from jax.experimental.pallas import tpu as pltpu
from jax.sharding import PartitionSpec as P

ROWS = 8
COST = {"last_sweep": 1}
LIMIT = {"edge_state": 62}


def call(kernel, name, **kw):
    us, limit = COST.get(name, 0), LIMIT.get(name, 24)
    return pl.pallas_call(
        kernel,
        compiler_params=pltpu.CompilerParams(vmem_limit_bytes=limit * 1024 * 1024),
        cost_estimate=pl.CostEstimate(flops=int(us * 1.1e9), bytes_accessed=0, transcendentals=0),
        name=name,
        **kw,
    )


def f32(*shape):
    return jax.ShapeDtypeStruct(shape, jnp.float32)


VMEM = pl.BlockSpec(memory_space=pltpu.VMEM)
SMEM = pl.BlockSpec(memory_space=pltpu.SMEM)
ANY = pl.BlockSpec(memory_space=pl.ANY)


def edge_of(slot, planes):
    up = lax.rem(lax.axis_index("slab") + slot, 2) == 0
    return jnp.where(up, planes - 1, 0)


def inverse_diag(c):
    return 1.0 / (0.5 + c(0) + 2.4 * (c(1) + c(2) + c(3)))


def shift_sum(p, axis):
    size = p.shape[axis]
    place = lax.broadcasted_iota(jnp.int32, p.shape, axis)
    ahead = jnp.where(place < size - 1, pltpu.roll(p, size - 1, axis), 0.0)
    behind = jnp.where(place > 0, pltpu.roll(p, 1, axis), 0.0)
    return ahead + behind


def edge_kernel(
    s_ref, c_ref, wall_ref, u0, u1, wsum_ref, s_buf, c_buf, wall_buf, c_sems, s_sems, wall_sem
):
    nv, nx = s_ref.shape[1:3]
    edges = [edge_of(slot, nx) for slot in (0, 1)]
    c_copies = [pltpu.make_async_copy(c_ref.at[0, :, e], c_buf.at[j], c_sems.at[j]) for j, e in enumerate(edges)]
    s_copies = [pltpu.make_async_copy(s_ref.at[0, :, e], s_buf.at[j], s_sems.at[j]) for j, e in enumerate(edges)]
    wall_copy = pltpu.make_async_copy(wall_ref.at[0], wall_buf, wall_sem)
    for j in (0, 1):
        c_copies[j].start()
        s_copies[j].start()
    wall_copy.start()
    for j, u in enumerate((u0, u1)):
        c_copies[j].wait()
        inv = inverse_diag(lambda k: c_buf[j, k])
        s_copies[j].wait()
        for v in range(nv):
            u[v] = s_buf[j, v] * inv
    wall_copy.wait()
    wall = jnp.sum(jnp.sum(wall_buf[...], axis=0, keepdims=True), axis=1, keepdims=True)
    rows = lax.broadcasted_iota(jnp.int32, wsum_ref.shape, 0)
    wsum_ref[...] = jnp.where(rows == lax.axis_index("node"), wall, 0.0)


def edge_state(source, coef, wall):
    nv, ny, nz = source.shape[1], source.shape[3], source.shape[4]
    return call(
        edge_kernel,
        "edge_state",
        out_shape=(f32(nv, ny, nz),) * 2 + (f32(ROWS, 128),),
        in_specs=[ANY] * 3,
        out_specs=(VMEM,) * 3,
        scratch_shapes=[
            pltpu.VMEM((2, nv, ny, nz), jnp.float32),
            pltpu.VMEM((2, 4, ny, nz), jnp.float32),
            pltpu.VMEM(wall.shape[1:], jnp.float32),
            pltpu.SemaphoreType.DMA((2,)),
            pltpu.SemaphoreType.DMA((2,)),
            pltpu.SemaphoreType.DMA,
        ],
    )(source, coef, wall)


def share(buf, parts, first, rows, part):
    width = buf.shape[1] // parts
    if parts == 1:
        return buf[pl.ds(first, rows), :]
    node = lax.axis_index("node")
    at = pl.multiple_of((node if part == 0 else 1 - node) * width, width)
    return buf[pl.ds(first, rows), pl.ds(at, width)]


def coupled(c_ref, x, below, here, above):
    q = c_ref[0, 1, x] * (below + above)
    q = q + c_ref[0, 2, x] * shift_sum(here, 0)
    return q + c_ref[0, 3, x] * shift_sum(here, 1)


def mixed(f_ref, w, q):
    mix = f_ref[0, 0, w] * q(0)
    for v in range(1, f_ref.shape[1]):
        mix = mix + f_ref[0, v, w] * q(v)
    return mix


def state_kernel(f_ref, s_ref, c_ref, after, out, part, q_ref, p_ref):
    del after
    nv, nx, ny, nz = s_ref.shape[1:]
    zero = jnp.zeros((ny, nz), jnp.float32)
    for slot in (0, 1):
        edge = edge_of(slot, nx)
        inner = jnp.where(edge == 0, 1, nx - 2)
        inv = inverse_diag(lambda k: c_ref[0, k, edge])
        inv_inner = inverse_diag(lambda k: c_ref[0, k, inner])
        for v in range(nv):
            p = s_ref[0, v, edge] * inv
            beside = s_ref[0, v, inner] * inv_inner
            q = coupled(c_ref, edge, beside, p, zero)
            if slot == 0:
                p_ref[v], q_ref[v] = p, q
            else:
                part[v], part[nv + v] = p, q * inv
        rho = c_ref[0, 1, edge] * inv
        if slot == 0:
            for w in range(nv):
                out[pl.ds(w * ny, ny), :] = p_ref[w] + inv * mixed(f_ref, w, lambda v: q_ref[v])
            out[pl.ds(nv * ny, ny), :] = rho
        else:
            part[2 * nv] = rho


def even_second(block, source, coef, after):
    nv, nx, ny, nz = source.shape[1:]
    return call(
        state_kernel,
        "even_second",
        out_shape=(f32((nv + 1) * ny, nz), f32(2 * nv + 1, ny, nz)),
        in_specs=[SMEM] + [VMEM] * 2 + [ANY],
        out_specs=(VMEM,) * 2,
        scratch_shapes=[pltpu.VMEM((nv, ny, nz), jnp.float32)] * 2,
    )(block, source, coef, after)


def odd_kernel(f_ref, part, after, out):
    del after
    nv, ny = f_ref.shape[1], part.shape[1]
    for w in range(nv):
        out[pl.ds(w * ny, ny), :] = part[w] + mixed(f_ref, w, lambda v: part[nv + v])
    out[pl.ds(nv * ny, ny), :] = part[2 * nv]


def odd_second(block, part, after):
    count, ny, nz = part.shape
    return call(
        odd_kernel,
        "odd_second",
        out_shape=f32((count + 1) // 2 * ny, nz),
        in_specs=[SMEM, VMEM, ANY],
        out_specs=VMEM,
    )(block, part, after)


def first_kernel(f_ref, s_ref, c_ref, m_ref, after, p1_ref, b_ref, sens_ref, p0, q_ref, inv_ref):
    del after
    nv, nx, ny, nz = s_ref.shape[1:]

    def start(x, _):
        inv = inverse_diag(lambda k: c_ref[0, k, x])
        inv_ref[x] = inv
        own = jnp.zeros((ny, nz), jnp.float32)
        for v in range(nv):
            p = s_ref[0, v, x] * inv
            p0[v, x] = p
            own = own + m_ref[0, v, x] * p
            q_ref[v] = m_ref[0, v, x] * inv
        sens_ref[pl.ds(x, 1), :] = jnp.sum(own, axis=0, keepdims=True)
        for v in range(nv):
            b = f_ref[0, v, 0] * q_ref[0]
            for w in range(1, nv):
                b = b + f_ref[0, v, w] * q_ref[w]
            b_ref[v, x] = b
        return 0

    lax.fori_loop(0, nx, start, 0)

    def first(x, _):
        for v in range(nv):
            q_ref[v] = coupled(c_ref, x, p0[v, x - 1], p0[v, x], p0[v, x + 1])
        for w in range(nv):
            p1_ref[w, x - 1] = p0[w, x] + inv_ref[x] * mixed(f_ref, w, lambda v: q_ref[v])
        return 0

    lax.fori_loop(1, nx - 1, first, 0)


def first_sweep(block, source, coef, metric, after):
    nv, nx, ny, nz = source.shape[1:]
    assert 2 < nx <= ROWS
    return call(
        first_kernel,
        "first_sweep",
        out_shape=(f32(nv, nx - 2, ny, nz), f32(nv, nx, ny, nz), f32(nx, nz)),
        in_specs=[SMEM] + [VMEM] * 3 + [ANY],
        out_specs=(VMEM,) * 3,
        scratch_shapes=[
            pltpu.VMEM((nv, nx, ny, nz), jnp.float32),
            pltpu.VMEM((nv, ny, nz), jnp.float32),
            pltpu.VMEM((nx, ny, nz), jnp.float32),
        ],
    )(block, source, coef, metric, after)


def weights_kernel(parts, f_ref, c_ref, b_ref, own_ref, after, weight_ref, *shares):
    del after
    nv, nx, ny, nz = b_ref.shape
    total = jnp.zeros((ny, nz), jnp.float32)
    for slot in (0, 1):
        edge = edge_of(slot, nx)
        for w in range(nv):
            weight = c_ref[0, 1, edge] * b_ref[w, edge]
            weight_ref[pl.ds((slot * nv + w) * ny, ny), :] = weight
            if slot == 1:
                total = total + weight * mixed(f_ref, w, lambda v: own_ref[v])
    weight_ref[pl.ds(2 * nv * ny, ny), :] = total
    for part, out in enumerate(shares):
        out[...] = share(weight_ref, parts, 0, nv * ny, part)


def edge_weights(parts, block, coef, b, own, after):
    nv, nx, ny, nz = b.shape
    rows = (2 * nv + 1) * ny
    return call(
        functools.partial(weights_kernel, parts),
        "edge_weights",
        out_shape=(f32(rows, nz),) + (f32(nv * ny, nz // parts),) * parts,
        in_specs=[SMEM] + [VMEM] * 3 + [ANY],
        out_specs=(VMEM,) * (1 + parts),
    )(block, coef, b, own, after)


def second_kernel(parts, f_ref, far0, far1, state0, state1, sums_ref, whole0, whole1, *msgs):
    nv, ny, nz = far0.shape
    rows = nv * ny
    for far, state, whole in ((far0, state0, whole0), (far1, state1, whole1)):
        rho = state[pl.ds(rows, ny), :]
        for w in range(nv):
            mix = mixed(f_ref, w, lambda v: far[v])
            whole[pl.ds(w * ny, ny), :] = state[pl.ds(w * ny, ny), :] + rho * mix
    for part, msg in enumerate(msgs):
        msg[pl.ds(0, rows), :] = share(whole0, parts, 0, rows, part)
        for k in range(msg.shape[1] // 128):
            msg[pl.ds(rows, ROWS), pl.ds(k * 128, 128)] = sums_ref[...]


def second_states(parts, block, far, states, sums):
    nv, ny, nz = far[0].shape
    return call(
        functools.partial(second_kernel, parts),
        "second_states",
        out_shape=(f32(nv * ny, nz),) * 2 + (f32(nv * ny + ROWS, nz // parts),) * parts,
        in_specs=[SMEM] + [VMEM] * 5,
        out_specs=(VMEM,) * (2 + parts),
    )(block, *far, *states, sums)


def last_kernel(c_ref, inner_ref, whole0, whole1, b_ref, base_ref, out_ref, p1):
    nv, nx, ny, nz = b_ref.shape
    zero = jnp.zeros((ny, nz), jnp.float32)
    for slot, whole in ((0, whole0), (1, whole1)):
        for v in range(nv):
            p1[v, edge_of(slot, nx)] = whole[pl.ds(v * ny, ny), :]

    def state(v, x):
        return inner_ref[v, x - 1] if 0 < x < nx - 1 else p1[v, x]

    for x in range(nx):
        along = [zero, zero, zero]
        for v in range(nv):
            b = b_ref[v, x]
            p = state(v, x)
            beside = [state(v, at) for at in (x - 1, x + 1) if 0 <= at < nx]
            along[0] = along[0] + b * sum(beside[1:], beside[0])
            along[1] = along[1] + b * shift_sum(p, 0)
            along[2] = along[2] + b * shift_sum(p, 1)
        own = c_ref[0, 1, x] * along[0] + c_ref[0, 2, x] * along[1] + c_ref[0, 3, x] * along[2]
        out_ref[x : x + 1, :] = base_ref[x : x + 1, :] + jnp.sum(own, axis=0, keepdims=True)


def last_sweep(coef, inner, edges, b, base):
    return call(
        last_kernel,
        "last_sweep",
        out_shape=f32(*base.shape),
        in_specs=[VMEM] * 6,
        out_specs=VMEM,
        scratch_shapes=[pltpu.VMEM(b.shape, jnp.float32)],
    )(coef, inner, *edges, b, base)


def factors(nodes, cells, sums):
    raw = [math.sin(math.pi * (n + 0.5) / nodes) for n in range(nodes)]
    weight = [r / sum(raw) for r in raw]
    objective = [sums[n : n + 1, :] * (1.0 / cells) for n in range(nodes)]
    mean = sum(w * o for w, o in zip(weight, objective))
    variance = sum(w * (o - mean) ** 2 for w, o in zip(weight, objective))
    spread = jnp.sqrt(variance + 0.25)
    return [w * (1.0 + 2.0 * (o - mean) / spread) for w, o in zip(weight, objective)]


def node_kernel(parts, few, sens_ref, weight_ref, odd_ref, *refs):
    sums, outs, acc = refs[:few], refs[few + 1 : -1], refs[-1]
    nx, nz = sens_ref.shape
    rows = odd_ref.shape[0]
    acc[...] = jnp.zeros_like(acc)
    acc[pl.ds(0, nx), :] = sens_ref[...]
    total = sums[0][...]
    for other in sums[1:]:
        total = total + other[...]
    for k in range(nz // 128):
        acc[pl.ds(ROWS, ROWS), pl.ds(k * 128, 128)] = total
    total = weight_ref[pl.ds(weight_ref.shape[0] - rows, rows), :] * odd_ref[...]
    acc[pl.ds(edge_of(1, nx), 1), :] += jnp.sum(total, axis=0, keepdims=True)
    for part, out in enumerate(outs):
        out[...] = share(acc, parts, 0, 2 * ROWS, part)


def node_terms(parts, sens, weight, odd, sums, after):
    nx, nz = sens.shape
    return call(
        functools.partial(node_kernel, parts, len(sums)),
        "node_terms",
        out_shape=(f32(2 * ROWS, nz // parts),) * parts,
        in_specs=[VMEM] * (3 + len(sums)) + [ANY],
        out_specs=(VMEM,) * parts,
        scratch_shapes=[pltpu.VMEM((2 * ROWS, nz), jnp.float32)],
    )(sens, weight, odd, *sums, after)


def gradient_kernel(parts, nodes, cells, *refs):
    terms, weights, msgs = (refs[k * parts : (k + 1) * parts] for k in range(3))
    out_ref, acc = refs[3 * parts :]
    nx = out_ref.shape[0]
    rows = weights[0].shape[0]
    sums = sum(r[pl.ds(at, ROWS), pl.ds(0, 128)] for refs, at in ((terms, ROWS), (msgs, rows)) for r in refs)
    factor = factors(nodes, cells, sums)
    node = lax.axis_index("node")
    out_ref[...] = jnp.zeros_like(out_ref)
    for part in range(parts):
        acc[...] = terms[part][pl.ds(0, ROWS), :]
        total = weights[part][...] * msgs[part][pl.ds(0, rows), :]
        acc[pl.ds(edge_of(0, nx), 1), :] += jnp.sum(total, axis=0, keepdims=True)
        whose = node if part == 0 else 1 - node
        scale = factor[0]
        for n in range(1, nodes):
            scale = jnp.where(whose == n, factor[n], scale)
        out_ref[...] += acc[pl.ds(0, nx), :] * scale[:, :1]


def gradient(nodes, cells, nx, terms, weights, msgs):
    parts, width = len(terms), terms[0].shape[1]
    return call(
        functools.partial(gradient_kernel, parts, nodes, cells),
        "gradient",
        out_shape=f32(nx, width),
        in_specs=[VMEM] * (3 * parts),
        out_specs=VMEM,
        scratch_shapes=[pltpu.VMEM((ROWS, width), jnp.float32)],
    )(*terms, *weights, *msgs)


def swap_pairs(value, slot, part=0):
    count, nodes = lax.axis_size("slab"), lax.axis_size("node")
    pairs = []
    for low in range(slot, count - 1, 2):
        pairs += [(low, low + 1), (low + 1, low)]
    if part == 0:
        return lax.ppermute(value, "slab", pairs)
    cross = [(n * count + a, (1 - n) * count + b) for n in range(nodes) for a, b in pairs]
    return lax.ppermute(value, ("node", "slab"), cross)


def from_partner(value, slab, node=0):
    count, nodes = lax.axis_size("slab"), lax.axis_size("node")
    pairs = [(n * count + i, (n ^ node) * count + (i ^ slab)) for n in range(nodes) for i in range(count)]
    return lax.ppermute(value, ("node", "slab"), pairs)


def other_core(value):
    return lax.ppermute(value, "node", [(0, 1), (1, 0)])


def after(value, *others):
    return lax.optimization_barrier((value, *others))[0]


def per_device(source, coef, block, metric, wall):
    nodes, slabs = lax.axis_size("node"), lax.axis_size("slab")
    nx = source.shape[2]
    cells = wall.shape[1] * slabs * wall.shape[2]
    parts = 2 if nodes == 2 else 1
    assert slabs & (slabs - 1) == 0 and slabs > 4
    *own, sums = edge_state(source, coef, wall)
    far = [swap_pairs(value, slot) for slot, value in enumerate(own)]
    inner, b, base = first_sweep(block, source, coef, metric, sums)
    first, *bits = [1 << k for k in range(1, slabs.bit_length() - 1)]
    sums = after(sums + from_partner(sums, first), base)
    even, part = even_second(block, source, coef, sums)
    for slab in bits[:-1]:
        sums = sums + from_partner(sums, slab)
    if parts == 1:
        sums = lax.psum(sums, "node")
    states = [even, odd_second(block, part, sums)]
    odd = swap_pairs(states[1], 1)
    edges = second_states(parts, block, far, states, sums)
    evens = [swap_pairs(value, 0, part) for part, value in enumerate(edges[2:])]
    sums = after(sums, edges[0])
    sums = [sums] + [from_partner(sums, bits[-1] ^ k) for k in (0, 1)]
    weight, *weights = edge_weights(parts, block, coef, b, own[1], states[1])
    weights[1:] = [other_core(value) for value in weights[1:]]
    sens = last_sweep(coef, inner, edges[:2], b, base)
    terms = list(node_terms(parts, sens, weight, odd, sums, weights[-1]))
    terms[1:] = [other_core(value) for value in terms[1:]]
    term = gradient(nodes, cells, nx, terms, weights, evens)
    if parts == 2:
        return term
    total = lax.psum(term, "node")
    width = total.shape[1] // nodes
    return lax.dynamic_slice_in_dim(total, lax.axis_index("node") * width, width, 1)


def solution(mesh):
    return jax.shard_map(
        per_device,
        mesh=mesh,
        in_specs=(
            P("node", None, "slab", None, None),
            P("node", None, "slab", None, None),
            P("node", None, None),
            P("node", None, "slab", None, None),
            P("node", "slab", None),
        ),
        out_specs=P("slab", "node"),
        check_vma=False,
    )
```

```python
import functools
import math

import jax
import jax.numpy as jnp
from jax import lax
from jax.experimental import pallas as pl
from jax.experimental.pallas import tpu as pltpu
from jax.sharding import PartitionSpec as P

ROWS = 8
COST = {"last_sweep": 1}
LIMIT = {"edge_state": 62}


def call(kernel, name, **kw):
    us, limit = COST.get(name, 0), LIMIT.get(name, 24)
    return pl.pallas_call(
        kernel,
        compiler_params=pltpu.CompilerParams(vmem_limit_bytes=limit * 1024 * 1024),
        cost_estimate=pl.CostEstimate(flops=int(us * 1.1e9), bytes_accessed=0, transcendentals=0),
        name=name,
        **kw,
    )


def f32(*shape):
    return jax.ShapeDtypeStruct(shape, jnp.float32)


VMEM = pl.BlockSpec(memory_space=pltpu.VMEM)
SMEM = pl.BlockSpec(memory_space=pltpu.SMEM)
ANY = pl.BlockSpec(memory_space=pl.ANY)


def edge_of(slot, planes):
    up = lax.rem(lax.axis_index("slab") + slot, 2) == 0
    return jnp.where(up, planes - 1, 0)


def inverse_diag(c):
    return 1.0 / (0.5 + c(0) + 2.4 * (c(1) + c(2) + c(3)))


def shift_sum(p, axis):
    size = p.shape[axis]
    place = lax.broadcasted_iota(jnp.int32, p.shape, axis)
    ahead = jnp.where(place < size - 1, pltpu.roll(p, size - 1, axis), 0.0)
    behind = jnp.where(place > 0, pltpu.roll(p, 1, axis), 0.0)
    return ahead + behind


def edge_kernel(
    s_ref, c_ref, wall_ref, u0, u1, wsum_ref, s_buf, c_buf, wall_buf, c_sems, s_sems, wall_sem
):
    nv, nx = s_ref.shape[1:3]
    edges = [edge_of(slot, nx) for slot in (0, 1)]
    c_copies = [pltpu.make_async_copy(c_ref.at[0, :, e], c_buf.at[j], c_sems.at[j]) for j, e in enumerate(edges)]
    s_copies = [pltpu.make_async_copy(s_ref.at[0, :, e], s_buf.at[j], s_sems.at[j]) for j, e in enumerate(edges)]
    wall_copy = pltpu.make_async_copy(wall_ref.at[0], wall_buf, wall_sem)
    for j in (0, 1):
        c_copies[j].start()
        s_copies[j].start()
    wall_copy.start()
    for j, u in enumerate((u0, u1)):
        c_copies[j].wait()
        inv = inverse_diag(lambda k: c_buf[j, k])
        s_copies[j].wait()
        for v in range(nv):
            u[v] = s_buf[j, v] * inv
    wall_copy.wait()
    wall = jnp.sum(jnp.sum(wall_buf[...], axis=0, keepdims=True), axis=1, keepdims=True)
    rows = lax.broadcasted_iota(jnp.int32, wsum_ref.shape, 0)
    wsum_ref[...] = jnp.where(rows == lax.axis_index("node"), wall, 0.0)


def edge_state(source, coef, wall):
    nv, ny, nz = source.shape[1], source.shape[3], source.shape[4]
    return call(
        edge_kernel,
        "edge_state",
        out_shape=(f32(nv, ny, nz),) * 2 + (f32(ROWS, 128),),
        in_specs=[ANY] * 3,
        out_specs=(VMEM,) * 3,
        scratch_shapes=[
            pltpu.VMEM((2, nv, ny, nz), jnp.float32),
            pltpu.VMEM((2, 4, ny, nz), jnp.float32),
            pltpu.VMEM(wall.shape[1:], jnp.float32),
            pltpu.SemaphoreType.DMA((2,)),
            pltpu.SemaphoreType.DMA((2,)),
            pltpu.SemaphoreType.DMA,
        ],
    )(source, coef, wall)


def share(buf, parts, first, rows, part):
    width = buf.shape[1] // parts
    if parts == 1:
        return buf[pl.ds(first, rows), :]
    node = lax.axis_index("node")
    at = pl.multiple_of((node if part == 0 else 1 - node) * width, width)
    return buf[pl.ds(first, rows), pl.ds(at, width)]


def coupled(c_ref, x, below, here, above):
    q = c_ref[0, 1, x] * (below + above)
    q = q + c_ref[0, 2, x] * shift_sum(here, 0)
    return q + c_ref[0, 3, x] * shift_sum(here, 1)


def mixed(f_ref, w, q):
    mix = f_ref[0, 0, w] * q(0)
    for v in range(1, f_ref.shape[1]):
        mix = mix + f_ref[0, v, w] * q(v)
    return mix


def state_kernel(f_ref, s_ref, c_ref, after, out, part, q_ref, p_ref):
    del after
    nv, nx, ny, nz = s_ref.shape[1:]
    zero = jnp.zeros((ny, nz), jnp.float32)
    for slot in (0, 1):
        edge = edge_of(slot, nx)
        inner = jnp.where(edge == 0, 1, nx - 2)
        inv = inverse_diag(lambda k: c_ref[0, k, edge])
        inv_inner = inverse_diag(lambda k: c_ref[0, k, inner])
        for v in range(nv):
            p = s_ref[0, v, edge] * inv
            beside = s_ref[0, v, inner] * inv_inner
            q = coupled(c_ref, edge, beside, p, zero)
            if slot == 0:
                p_ref[v], q_ref[v] = p, q
            else:
                part[v], part[nv + v] = p, q * inv
        rho = c_ref[0, 1, edge] * inv
        if slot == 0:
            for w in range(nv):
                out[pl.ds(w * ny, ny), :] = p_ref[w] + inv * mixed(f_ref, w, lambda v: q_ref[v])
            out[pl.ds(nv * ny, ny), :] = rho
        else:
            part[2 * nv] = rho
            for w in range(nv // 2):
                part[w] = part[w] + mixed(f_ref, w, lambda v: part[nv + v])


def even_second(block, source, coef, after):
    nv, nx, ny, nz = source.shape[1:]
    return call(
        state_kernel,
        "even_second",
        out_shape=(f32((nv + 1) * ny, nz), f32(2 * nv + 1, ny, nz)),
        in_specs=[SMEM] + [VMEM] * 2 + [ANY],
        out_specs=(VMEM,) * 2,
        scratch_shapes=[pltpu.VMEM((nv, ny, nz), jnp.float32)] * 2,
    )(block, source, coef, after)


def odd_kernel(f_ref, part, after, out):
    del after
    nv, ny = f_ref.shape[1], part.shape[1]
    for w in range(nv):
        mix = mixed(f_ref, w, lambda v: part[nv + v]) if w >= nv // 2 else 0.0
        out[pl.ds(w * ny, ny), :] = part[w] + mix
    out[pl.ds(nv * ny, ny), :] = part[2 * nv]


def odd_second(block, part, after):
    count, ny, nz = part.shape
    return call(
        odd_kernel,
        "odd_second",
        out_shape=f32((count + 1) // 2 * ny, nz),
        in_specs=[SMEM, VMEM, ANY],
        out_specs=VMEM,
    )(block, part, after)


def first_kernel(f_ref, s_ref, c_ref, m_ref, after, p1_ref, b_ref, sens_ref, p0, q_ref, inv_ref):
    del after
    nv, nx, ny, nz = s_ref.shape[1:]

    def start(x, _):
        inv = inverse_diag(lambda k: c_ref[0, k, x])
        inv_ref[x] = inv
        own = jnp.zeros((ny, nz), jnp.float32)
        for v in range(nv):
            p = s_ref[0, v, x] * inv
            p0[v, x] = p
            own = own + m_ref[0, v, x] * p
            q_ref[v] = m_ref[0, v, x] * inv
        sens_ref[pl.ds(x, 1), :] = jnp.sum(own, axis=0, keepdims=True)
        for v in range(nv):
            b = f_ref[0, v, 0] * q_ref[0]
            for w in range(1, nv):
                b = b + f_ref[0, v, w] * q_ref[w]
            b_ref[v, x] = b
        return 0

    lax.fori_loop(0, nx, start, 0)

    def first(x, _):
        for v in range(nv):
            q_ref[v] = coupled(c_ref, x, p0[v, x - 1], p0[v, x], p0[v, x + 1])
        for w in range(nv):
            p1_ref[w, x - 1] = p0[w, x] + inv_ref[x] * mixed(f_ref, w, lambda v: q_ref[v])
        return 0

    lax.fori_loop(1, nx - 1, first, 0)


def first_sweep(block, source, coef, metric, after):
    nv, nx, ny, nz = source.shape[1:]
    assert 2 < nx <= ROWS
    return call(
        first_kernel,
        "first_sweep",
        out_shape=(f32(nv, nx - 2, ny, nz), f32(nv, nx, ny, nz), f32(nx, nz)),
        in_specs=[SMEM] + [VMEM] * 3 + [ANY],
        out_specs=(VMEM,) * 3,
        scratch_shapes=[
            pltpu.VMEM((nv, nx, ny, nz), jnp.float32),
            pltpu.VMEM((nv, ny, nz), jnp.float32),
            pltpu.VMEM((nx, ny, nz), jnp.float32),
        ],
    )(block, source, coef, metric, after)


def weights_kernel(parts, f_ref, c_ref, b_ref, own_ref, after, weight_ref, *shares):
    del after
    nv, nx, ny, nz = b_ref.shape
    total = jnp.zeros((ny, nz), jnp.float32)
    for slot in (0, 1):
        edge = edge_of(slot, nx)
        for w in range(nv):
            weight = c_ref[0, 1, edge] * b_ref[w, edge]
            weight_ref[pl.ds((slot * nv + w) * ny, ny), :] = weight
            if slot == 1:
                total = total + weight * mixed(f_ref, w, lambda v: own_ref[v])
    weight_ref[pl.ds(2 * nv * ny, ny), :] = total
    for part, out in enumerate(shares):
        out[...] = share(weight_ref, parts, 0, nv * ny, part)


def edge_weights(parts, block, coef, b, own, after):
    nv, nx, ny, nz = b.shape
    rows = (2 * nv + 1) * ny
    return call(
        functools.partial(weights_kernel, parts),
        "edge_weights",
        out_shape=(f32(rows, nz),) + (f32(nv * ny, nz // parts),) * parts,
        in_specs=[SMEM] + [VMEM] * 3 + [ANY],
        out_specs=(VMEM,) * (1 + parts),
    )(block, coef, b, own, after)


def second_kernel(parts, f_ref, far0, far1, state0, state1, sums_ref, whole0, whole1, *msgs):
    nv, ny, nz = far0.shape
    rows = nv * ny
    for far, state, whole in ((far0, state0, whole0), (far1, state1, whole1)):
        rho = state[pl.ds(rows, ny), :]
        for w in range(nv):
            mix = mixed(f_ref, w, lambda v: far[v])
            whole[pl.ds(w * ny, ny), :] = state[pl.ds(w * ny, ny), :] + rho * mix
    for part, msg in enumerate(msgs):
        msg[pl.ds(0, rows), :] = share(whole0, parts, 0, rows, part)
        for k in range(msg.shape[1] // 128):
            msg[pl.ds(rows, ROWS), pl.ds(k * 128, 128)] = sums_ref[...]


def second_states(parts, block, far, states, sums):
    nv, ny, nz = far[0].shape
    return call(
        functools.partial(second_kernel, parts),
        "second_states",
        out_shape=(f32(nv * ny, nz),) * 2 + (f32(nv * ny + ROWS, nz // parts),) * parts,
        in_specs=[SMEM] + [VMEM] * 5,
        out_specs=(VMEM,) * (2 + parts),
    )(block, *far, *states, sums)


def last_kernel(c_ref, inner_ref, whole0, whole1, b_ref, base_ref, out_ref, p1):
    nv, nx, ny, nz = b_ref.shape
    zero = jnp.zeros((ny, nz), jnp.float32)
    for slot, whole in ((0, whole0), (1, whole1)):
        for v in range(nv):
            p1[v, edge_of(slot, nx)] = whole[pl.ds(v * ny, ny), :]

    def state(v, x):
        return inner_ref[v, x - 1] if 0 < x < nx - 1 else p1[v, x]

    for x in range(nx):
        along = [zero, zero, zero]
        for v in range(nv):
            b = b_ref[v, x]
            p = state(v, x)
            beside = [state(v, at) for at in (x - 1, x + 1) if 0 <= at < nx]
            along[0] = along[0] + b * sum(beside[1:], beside[0])
            along[1] = along[1] + b * shift_sum(p, 0)
            along[2] = along[2] + b * shift_sum(p, 1)
        own = c_ref[0, 1, x] * along[0] + c_ref[0, 2, x] * along[1] + c_ref[0, 3, x] * along[2]
        out_ref[x : x + 1, :] = base_ref[x : x + 1, :] + jnp.sum(own, axis=0, keepdims=True)


def last_sweep(coef, inner, edges, b, base):
    return call(
        last_kernel,
        "last_sweep",
        out_shape=f32(*base.shape),
        in_specs=[VMEM] * 6,
        out_specs=VMEM,
        scratch_shapes=[pltpu.VMEM(b.shape, jnp.float32)],
    )(coef, inner, *edges, b, base)


def factors(nodes, cells, sums):
    raw = [math.sin(math.pi * (n + 0.5) / nodes) for n in range(nodes)]
    weight = [r / sum(raw) for r in raw]
    objective = [sums[n : n + 1, :] * (1.0 / cells) for n in range(nodes)]
    mean = sum(w * o for w, o in zip(weight, objective))
    variance = sum(w * (o - mean) ** 2 for w, o in zip(weight, objective))
    spread = jnp.sqrt(variance + 0.25)
    return [w * (1.0 + 2.0 * (o - mean) / spread) for w, o in zip(weight, objective)]


def node_kernel(parts, few, sens_ref, weight_ref, odd_ref, *refs):
    sums, outs, acc = refs[:few], refs[few + 1 : -1], refs[-1]
    nx, nz = sens_ref.shape
    rows = odd_ref.shape[0]
    acc[...] = jnp.zeros_like(acc)
    acc[pl.ds(0, nx), :] = sens_ref[...]
    total = sums[0][...]
    for other in sums[1:]:
        total = total + other[...]
    for k in range(nz // 128):
        acc[pl.ds(ROWS, ROWS), pl.ds(k * 128, 128)] = total
    total = weight_ref[pl.ds(weight_ref.shape[0] - rows, rows), :] * odd_ref[...]
    acc[pl.ds(edge_of(1, nx), 1), :] += jnp.sum(total, axis=0, keepdims=True)
    for part, out in enumerate(outs):
        out[...] = share(acc, parts, 0, 2 * ROWS, part)


def node_terms(parts, sens, weight, odd, sums, after):
    nx, nz = sens.shape
    return call(
        functools.partial(node_kernel, parts, len(sums)),
        "node_terms",
        out_shape=(f32(2 * ROWS, nz // parts),) * parts,
        in_specs=[VMEM] * (3 + len(sums)) + [ANY],
        out_specs=(VMEM,) * parts,
        scratch_shapes=[pltpu.VMEM((2 * ROWS, nz), jnp.float32)],
    )(sens, weight, odd, *sums, after)


def gradient_kernel(parts, nodes, cells, *refs):
    terms, weights, msgs = (refs[k * parts : (k + 1) * parts] for k in range(3))
    out_ref, acc = refs[3 * parts :]
    nx = out_ref.shape[0]
    rows = weights[0].shape[0]
    sums = sum(r[pl.ds(at, ROWS), pl.ds(0, 128)] for refs, at in ((terms, ROWS), (msgs, rows)) for r in refs)
    factor = factors(nodes, cells, sums)
    node = lax.axis_index("node")
    out_ref[...] = jnp.zeros_like(out_ref)
    for part in range(parts):
        acc[...] = terms[part][pl.ds(0, ROWS), :]
        total = weights[part][...] * msgs[part][pl.ds(0, rows), :]
        acc[pl.ds(edge_of(0, nx), 1), :] += jnp.sum(total, axis=0, keepdims=True)
        whose = node if part == 0 else 1 - node
        scale = factor[0]
        for n in range(1, nodes):
            scale = jnp.where(whose == n, factor[n], scale)
        out_ref[...] += acc[pl.ds(0, nx), :] * scale[:, :1]


def gradient(nodes, cells, nx, terms, weights, msgs):
    parts, width = len(terms), terms[0].shape[1]
    return call(
        functools.partial(gradient_kernel, parts, nodes, cells),
        "gradient",
        out_shape=f32(nx, width),
        in_specs=[VMEM] * (3 * parts),
        out_specs=VMEM,
        scratch_shapes=[pltpu.VMEM((ROWS, width), jnp.float32)],
    )(*terms, *weights, *msgs)


def swap_pairs(value, slot, part=0):
    count, nodes = lax.axis_size("slab"), lax.axis_size("node")
    pairs = []
    for low in range(slot, count - 1, 2):
        pairs += [(low, low + 1), (low + 1, low)]
    if part == 0:
        return lax.ppermute(value, "slab", pairs)
    cross = [(n * count + a, (1 - n) * count + b) for n in range(nodes) for a, b in pairs]
    return lax.ppermute(value, ("node", "slab"), cross)


def from_partner(value, slab, node=0):
    count, nodes = lax.axis_size("slab"), lax.axis_size("node")
    pairs = [(n * count + i, (n ^ node) * count + (i ^ slab)) for n in range(nodes) for i in range(count)]
    return lax.ppermute(value, ("node", "slab"), pairs)


def other_core(value):
    return lax.ppermute(value, "node", [(0, 1), (1, 0)])


def after(value, *others):
    return lax.optimization_barrier((value, *others))[0]


def per_device(source, coef, block, metric, wall):
    nodes, slabs = lax.axis_size("node"), lax.axis_size("slab")
    nx = source.shape[2]
    cells = wall.shape[1] * slabs * wall.shape[2]
    parts = 2 if nodes == 2 else 1
    assert slabs & (slabs - 1) == 0 and slabs > 4
    *own, sums = edge_state(source, coef, wall)
    far = [swap_pairs(value, slot) for slot, value in enumerate(own)]
    inner, b, base = first_sweep(block, source, coef, metric, sums)
    first, *bits = [1 << k for k in range(1, slabs.bit_length() - 1)]
    sums = after(sums + from_partner(sums, first), base)
    even, part = even_second(block, source, coef, sums)
    for slab in bits[:-1]:
        sums = sums + from_partner(sums, slab)
    if parts == 1:
        sums = lax.psum(sums, "node")
    states = [even, odd_second(block, part, sums)]
    odd = swap_pairs(states[1], 1)
    edges = second_states(parts, block, far, states, sums)
    evens = [swap_pairs(value, 0, part) for part, value in enumerate(edges[2:])]
    sums = after(sums, edges[0])
    sums = [sums] + [from_partner(sums, bits[-1] ^ k) for k in (0, 1)]
    weight, *weights = edge_weights(parts, block, coef, b, own[1], states[1])
    weights[1:] = [other_core(value) for value in weights[1:]]
    sens = last_sweep(coef, inner, edges[:2], b, base)
    terms = list(node_terms(parts, sens, weight, odd, sums, weights[-1]))
    terms[1:] = [other_core(value) for value in terms[1:]]
    term = gradient(nodes, cells, nx, terms, weights, evens)
    if parts == 2:
        return term
    total = lax.psum(term, "node")
    width = total.shape[1] // nodes
    return lax.dynamic_slice_in_dim(total, lax.axis_index("node") * width, width, 1)


def solution(mesh):
    return jax.shard_map(
        per_device,
        mesh=mesh,
        in_specs=(
            P("node", None, "slab", None, None),
            P("node", None, "slab", None, None),
            P("node", None, None),
            P("node", None, "slab", None, None),
            P("node", "slab", None),
        ),
        out_specs=P("slab", "node"),
        check_vma=False,
    )
```
